128 devices in a mesh: dp: 4 (over z), expert: 32 (over y, x, core).
Axes of the slice: x: 4, y: 4, z: 4, core: 2. Of those that a mesh axis runs over, the one named last changes fastest.
Arguments:
- tokens: bfloat16 [16384, 2048], P(('dp', 'expert')), may hold values from -6 to 6
- expert_ids: int32 [16384, 8], P(('dp', 'expert')), may hold values from 0 to 63, all different within a row; in each aligned block of 128 rows (0 to 127, 128 to 255, ...) at most 20 rows name the same one
- gate_scores: float32 [16384, 8], P(('dp', 'expert')), may hold values from 0.05 to 1
- w_in: bfloat16 [64, 2048, 1536], P('expert'), may hold values from -0.125 to 0.125
- w_out: bfloat16 [64, 768, 2048], P('expert'), may hold values from -0.21875 to 0.21875
- cotangent: bfloat16 [16384, 2048], P(('dp', 'expert')), may hold values from -6 to 6
Outputs:
- mixed: bfloat16 [16384, 2048], P(('dp', 'expert'))
- score_grad: float32 [16384, 8], P(('dp', 'expert'))
- grad_in: bfloat16 [64, 2048, 1536], P('expert', 'dp')
- grad_out: bfloat16 [64, 768, 2048], P('expert', None, 'dp')
The draws below stay inside these ranges and needn't reach their ends.
Inputs may be any that keep to these rules, and one draw needn't show every extreme that they name: `expert_ids`: each token names 8 different experts. Among the 128 tokens of one device no expert is named by more than 20 tokens, and in some device's tokens an expert is named by exactly 20. Every expert is named by some token.
All inputs are finite; a program needn't handle non-finite values.
Results may differ from the reference program's by a relative error of at most 0.013.
Values may be sent and summed in bfloat16 or wider, within the bound.
A program may use at most 256 MiB of HBM per device.

```python
import math
import jax
import jax.numpy as jnp
import numpy as np
from jax import lax

D = 2048
FF = 768
TOPK = 8
TOK_DEV = 128
EXPERTS = 64
TOKENS = 16384
MOST = 20
N_DP = 4
N_EXPERT = 32


def level_of(key, shape, split, smallest, largest):
    gain, own = 1.0, jax.random.fold_in(key, 6)
    for position, blocks in split:
        steps = jnp.exp(jax.random.uniform(jax.random.fold_in(own, position), (blocks,), jnp.float32, smallest / len(split), largest / len(split)))
        gain = gain * jnp.repeat(steps, shape[position] // blocks).reshape([-1 if axis == position else 1 for axis in range(len(shape))])
    return gain


def shared_out(own_key, own, number, rows, amount, top, limit, slope):
    sequence = jax.random.permutation(own_key, amount)
    heavy_load, common = load_shares(amount, rows * top, limit, slope, True), load_shares(amount, rows * top, limit, slope, False)
    places = jnp.arange(amount)

    def named(lengths, rotation):
        used = int((lengths > 0).sum())
        fixed = max(1, used // 4)
        passed = fixed + (places - fixed + rotation * (used - fixed)) % max(1, amount - fixed)
        return jnp.zeros((amount,), jnp.int32).at[sequence[jnp.where(places < fixed, places, passed)]].set(jnp.asarray(lengths, jnp.int32))

    lengths = jnp.where(number % 4 == 0, named(heavy_load, number // 4), named(common, number - number // 4 - 1))
    mixed = jax.random.permutation(jax.random.fold_in(own, 3), amount)
    giver, sink = mixed[0:amount // 2 * 2:2], mixed[1:amount // 2 * 2:2]
    margin = jnp.minimum(lengths[giver] - 1, limit - lengths[sink]) // 2
    margin = jnp.where((giver == sequence[0]) | (sink == sequence[0]) | (lengths[sink] == 0), 0, jnp.maximum(margin, 0))
    passed = jax.random.randint(jax.random.fold_in(own, 4), (amount // 2,), 0, 1 << 20) % (margin + 1)
    lengths = lengths.at[giver].add(-passed).at[sink].add(passed)
    labels = jnp.searchsorted(jnp.cumsum(lengths), jnp.arange(rows * top), side="right").astype(jnp.int32)
    listing = labels.reshape(top, rows).T
    listing = listing[jax.random.permutation(jax.random.fold_in(own, 1), rows)]
    rotation = jax.random.randint(jax.random.fold_in(own, 2), (rows, 1), 0, top)
    return jnp.take_along_axis(listing, (jnp.arange(top)[None, :] + rotation) % top, axis=1)


def load_shares(number_of, total, bound, lean, full):
    loads = [(1 << 20) // math.isqrt(rank ** lean) + 1 for rank in range(1, number_of + 1)]
    largest = bound if full else min(bound, max(-(-total // number_of), total * loads[0] // sum(loads)))
    least = 1 if total - largest >= number_of - 1 else 0
    counts, surplus = [largest] + [least] * (number_of - 1), total - largest - least * (number_of - 1)
    while surplus > 0:
        movable = [i for i in range(1, number_of) if counts[i] < largest] or [i for i in range(1, number_of) if counts[i] < bound]
        mass, remaining = sum([loads[i] for i in movable]), surplus
        for i in movable:
            addition = min(bound - counts[i], max(1, remaining * loads[i] // mass), surplus)
            counts[i] = counts[i] + addition
            surplus = surplus - addition
    return np.array(counts)


def scatter_about(rng, dims, spread, most, shards=(), held_as=jnp.bfloat16):
    result = spread * jax.random.normal(rng, dims, jnp.float32)
    if shards:
        result = result * level_of(rng, dims, shards, -0.22, 0.18)
    return jnp.clip(result, -most, most).astype(held_as)


def setup_inputs(seed: int = 0) -> dict:
    key_list = jax.random.split(jax.random.key(seed), 7)
    tokens = scatter_about(key_list[0], (TOKENS, D), 1.0, 6.0, ((0, 128),))
    expert_ids_keys = jax.random.split(jax.random.fold_in(key_list[1], 1), TOKENS // TOK_DEV)
    expert_ids_turns = jax.random.permutation(jax.random.fold_in(key_list[1], 3), TOKENS // TOK_DEV)
    expert_ids = jax.vmap(lambda own, number: shared_out(jax.random.fold_in(key_list[1], 2), own, number, TOK_DEV, EXPERTS, TOPK, MOST, 2))(expert_ids_keys, expert_ids_turns).reshape((TOKENS, TOPK))
    gate_scores = jnp.clip(jnp.exp(math.log(1.0) - 2.9957323 * jax.random.uniform(key_list[2], (TOKENS, TOPK), jnp.float32) ** level_of(key_list[2], (TOKENS, TOPK), ((0, 128),), -0.2, 0.2)), 0.05, 1.0)
    w_in = scatter_about(key_list[3], (EXPERTS, D, 2 * FF), D ** -0.5, 0.125, ((0, 32),))
    w_out = scatter_about(key_list[4], (EXPERTS, FF, D), FF ** -0.5, 0.21875, ((0, 32),))
    cotangent = scatter_about(key_list[5], (TOKENS, D), 1.0, 6.0, ((0, 128),))
    return dict(tokens=tokens, expert_ids=expert_ids, gate_scores=gate_scores, w_in=w_in, w_out=w_out, cotangent=cotangent)


def slot_plan(flat):
    onehot = (flat[:, None] == jnp.arange(EXPERTS, dtype=jnp.int32)[None, :]).astype(jnp.int32)
    before = jnp.cumsum(onehot, axis=0) - onehot
    slot = jnp.sum(before * onehot, axis=1).astype(jnp.int32)
    place = (flat * MOST + slot).astype(jnp.int32)
    source = jnp.full((EXPERTS * MOST,), -1, jnp.int32).at[place].set(jnp.arange(flat.shape[0], dtype=jnp.int32))
    return source


def reference(tokens, expert_ids, gate_scores, w_in, w_out, cotangent):
    blocks = N_DP * N_EXPERT
    assigned = TOK_DEV * TOPK
    flat_ids = expert_ids.reshape(blocks, assigned).astype(jnp.int32)
    source = jax.vmap(slot_plan)(flat_ids)
    offsets = (jnp.arange(blocks, dtype=jnp.int32) * assigned)[:, None]
    globe = jnp.where(source >= 0, source + offsets, -1).astype(jnp.int32)
    globe = globe.reshape(N_DP, N_EXPERT, EXPERTS, MOST).transpose(2, 0, 1, 3).reshape(EXPERTS, N_DP, N_EXPERT * MOST)
    total = jnp.sum(gate_scores, axis=1, keepdims=True)
    weights = gate_scores / total
    weight_flat = weights.reshape(-1)
    rows = N_EXPERT * MOST

    def step(carry, inputs):
        mixed_acc, affinity = carry
        index, w_gu, w_o = inputs
        valid = index >= 0
        safe = jnp.maximum(index, 0)
        tok = safe // TOPK
        x_rows = jnp.where(valid[..., None], tokens[tok], jnp.zeros((), jnp.bfloat16))
        x_flat = x_rows.reshape(N_DP * rows, D)
        gate_up = jnp.dot(x_flat, w_gu, preferred_element_type=jnp.float32)
        gate = gate_up[:, :FF]
        up = gate_up[:, FF:]
        sig = jax.nn.sigmoid(gate)
        silu = gate * sig
        hidden = (silu * up).astype(jnp.bfloat16)
        produced = jnp.dot(hidden, w_o, preferred_element_type=jnp.float32).astype(jnp.bfloat16)
        valid_flat = valid.reshape(-1)
        safe_flat = safe.reshape(-1)
        tok_flat = tok.reshape(-1)
        wrow = weight_flat[safe_flat]
        dy_rows = jnp.where(valid_flat[:, None], cotangent[tok_flat], jnp.zeros((), jnp.bfloat16))
        out_grad = (wrow[:, None] * dy_rows.astype(jnp.float32)).astype(jnp.bfloat16)
        g_rows = jnp.sum(produced.astype(jnp.float32) * dy_rows.astype(jnp.float32), axis=1)
        hidden_grad = jnp.dot(out_grad, w_o.T, preferred_element_type=jnp.float32)
        d_gate = hidden_grad * up * sig * (1.0 + gate * (1.0 - sig))
        d_up = hidden_grad * silu
        gu_grad = jnp.concatenate([d_gate, d_up], axis=1).astype(jnp.bfloat16)
        zero = jnp.zeros((), jnp.float32)
        mixed_acc = mixed_acc.at[tok_flat].add(jnp.where(valid_flat[:, None], wrow[:, None] * produced.astype(jnp.float32), zero))
        affinity = affinity.at[safe_flat].add(jnp.where(valid_flat, g_rows, zero))
        xb = x_rows.astype(jnp.float32)
        gb = gu_grad.reshape(N_DP, rows, 2 * FF).astype(jnp.float32)
        hb = hidden.reshape(N_DP, rows, FF).astype(jnp.float32)
        ob = out_grad.reshape(N_DP, rows, D).astype(jnp.float32)
        term_in = jnp.einsum('brd,brf->bdf', xb, gb, precision=lax.Precision.HIGHEST)
        term_out = jnp.einsum('brf,brd->bfd', hb, ob, precision=lax.Precision.HIGHEST)
        term_in = lax.optimization_barrier(term_in.astype(jnp.bfloat16)).astype(jnp.float32)
        term_out = lax.optimization_barrier(term_out.astype(jnp.bfloat16)).astype(jnp.float32)
        grad_w_in = jnp.sum(term_in, axis=0).astype(jnp.bfloat16)
        grad_w_out = jnp.sum(term_out, axis=0).astype(jnp.bfloat16)
        return (mixed_acc, affinity), (grad_w_in, grad_w_out)

    start = (jnp.zeros((TOKENS, D), jnp.float32), jnp.zeros((TOKENS * TOPK,), jnp.float32))
    carry, stacked = lax.scan(step, start, (globe, w_in, w_out))
    mixed_acc, affinity = carry
    affinity = affinity.reshape(TOKENS, TOPK)
    score_grad = (affinity - jnp.sum(weights * affinity, axis=1, keepdims=True)) / total
    return mixed_acc.astype(jnp.bfloat16), score_grad, stacked[0], stacked[1]
```

```python
import functools

import jax
import jax.numpy as jnp
from jax import lax
from jax.experimental import pallas as pl
from jax.experimental.pallas import tpu as pltpu
from jax.sharding import PartitionSpec as P

MESH = pl.DeviceIdType.MESH
BF = jnp.bfloat16
F32 = jnp.float32

TOK = 128
D = 2048
FF = 768
PEERS = 32
MAIN = 16
GRP = 512
BLK = 80
ROWS = PEERS * 20
AREA = PEERS * BLK
UROWS = 384 + 3 * 256
BATCH = 16


def dot(a, b, dims=((1,), (0,))):
    return lax.dot_general(a, b, (dims, ((), ())), preferred_element_type=F32)


def peer(me, i):
    c = lax.rem(me, 2)
    x = lax.rem(lax.div(me, 2), 4)
    y = lax.div(me, 8)
    dc = lax.rem(i, 2)
    dx = lax.rem(lax.div(i, 2), 4)
    dy = lax.div(i, 8)
    return lax.rem(y + dy, 4) * 8 + lax.rem(x + dx, 4) * 2 + lax.rem(c + dc, 2)


def turn(me, i):
    return peer(me, lax.rem(i * 11, PEERS))


def iota(shape, dim):
    return lax.broadcasted_iota(jnp.int32, shape, dim)


def rows_of(p):
    if isinstance(p, int):
        return (0, 384) if p == 0 else (384 + 256 * (p - 1), 256)
    return (pl.multiple_of(384 + 256 * (p - 1), 128), 256)


def kernel(
    tok, cot, ids, scores, win_hbm, wout_hbm,
    mixed, score, gin, gout, back, parts,
    big, recv, win, wout, xs, xt, ht, hid, gate, up, gg, stage, slot, wgt, cut, perm, perm_t,
    over, side, slot4, wgt4, aff, macc,
    d_send, d_recv, r_send, r_recv, z_send, z_recv, l_sem, w_sem, o_sem,
):
    b = lax.axis_index("dp")
    me = lax.axis_index("expert")
    right = lax.rem(b + 1, 4)
    left = lax.rem(b + 3, 4)

    def load_in(j):
        return pltpu.make_async_copy(win_hbm.at[j], win, w_sem.at[0])

    def load_out(j):
        return pltpu.make_async_copy(wout_hbm.at[j], wout, w_sem.at[1])

    load_in(0).start()
    load_out(0).start()

    barrier = pltpu.get_barrier_semaphore()

    def greet(i, _):
        pl.semaphore_signal(barrier, inc=1, device_id=(b, peer(me, i)), device_id_type=MESH)
        return 0

    lax.fori_loop(1, PEERS, greet, 0)
    pl.semaphore_signal(barrier, inc=1, device_id=(right, me), device_id_type=MESH)
    pl.semaphore_signal(barrier, inc=1, device_id=(left, me), device_id_type=MESH)

    names = ids[...]
    total = jnp.sum(scores[...], axis=0, keepdims=True)
    weights = scores[...] / total
    row = iota((64, TOK), 0)
    expert = 2 * lax.rem(row, PEERS) + lax.div(row, PEERS)
    member = jnp.zeros((64, TOK), F32)
    weight = jnp.zeros((64, TOK), F32)
    for k in range(8):
        hit = names[k : k + 1, :] == expert
        member = member + jnp.where(hit, 1.0, 0.0)
        weight = weight + jnp.where(hit, weights[k : k + 1, :], 0.0)
    earlier = jnp.where(iota((TOK, TOK), 0) < iota((TOK, TOK), 1), 1.0, 0.0).astype(BF)
    slot[...] = jnp.where(member > 0.0, dot(member.astype(BF), earlier), -1.0)
    wgt[...] = weight

    r0, r1 = iota((GRP, GRP), 0), iota((GRP, GRP), 1)

    def place(m):
        r = lax.rem(m, 128)
        return 16 * lax.div(r, 4) + 4 * lax.div(m, 128) + lax.rem(r, 4)

    perm[...] = jnp.where(r1 == place(r0), 1.0, 0.0).astype(BF)
    perm_t[...] = jnp.where(r0 == place(r1), 1.0, 0.0).astype(BF)

    main_slot = iota((MAIN, TOK), 0).astype(F32)
    over_row = iota((MAIN, TOK), 0)
    over_slot = (16 + lax.rem(over_row, 4)).astype(F32)
    over_group = lax.div(over_row, 4)

    def block(q):
        return pl.ds(pl.multiple_of(q * BLK, 16), BLK)

    def send_block(j, a, q):
        return big.at[j, pl.ds(pl.multiple_of(a * AREA + q * BLK, 16), BLK)]

    def dispatch_copy(j, a, q, lands):
        return pltpu.make_async_remote_copy(
            src_ref=send_block(j, a, q),
            dst_ref=recv.at[2 * j + a, block(lands)],
            send_sem=d_send.at[2 * j + a, q],
            recv_sem=d_recv.at[2 * j + a, lands],
            device_id=(b, q),
            device_id_type=MESH,
        )

    def own_copy(j, a):
        return pltpu.make_async_copy(
            send_block(j, a, me), recv.at[2 * j + a, block(me)], l_sem.at[2 * j + a]
        )

    def dispatch(j, a):
        source = (tok, cot)[a]

        def batch(g, _):
            hots, overs, w_main, w_over = [], [], [], []
            for u in range(BATCH):
                q = turn(me, g * BATCH + u)
                mine = slot[pl.ds(j * PEERS + q, 1), :]
                hot = jnp.where(main_slot == mine, 1.0, 0.0)
                hot4 = jnp.where(over_slot == mine, 1.0, 0.0)
                hots.append(hot)
                overs.append(
                    jnp.concatenate(
                        [jnp.where(over_group == c, hot4, 0.0) for c in range(4)], axis=1
                    )
                )
                if a == 1:
                    heavy = wgt[pl.ds(j * PEERS + q, 1), :]
                    w_main.append(jnp.sum(hot * heavy, axis=1, keepdims=True))
                    w_over.append(jnp.sum(hot4 * heavy, axis=1, keepdims=True))
            pick = jnp.concatenate(hots, axis=0).astype(BF)
            pick4 = jnp.concatenate(overs, axis=0).astype(BF)
            scale = jnp.concatenate(w_main, axis=0) if a == 1 else None
            scale4 = jnp.concatenate(w_over, axis=0) if a == 1 else None
            extra = None
            for c in range(4):
                columns = source[:, c * GRP : (c + 1) * GRP]
                rows = dot(pick, columns)
                more = dot(pick4[:, c * TOK : (c + 1) * TOK], columns)
                extra = more if extra is None else extra + more
                if a == 1:
                    rows = rows * scale
                rows = rows.astype(BF)
                for u in range(BATCH):
                    q = turn(me, g * BATCH + u)
                    at = pl.multiple_of(a * AREA + q * BLK + 16 * c, 16)
                    big[j, pl.ds(at, 16), :] = rows[u * 16 : u * 16 + 16, :]
            if a == 1:
                extra = extra * scale4
            extra = extra.astype(BF)
            for u in range(BATCH):
                q = turn(me, g * BATCH + u)
                at = pl.multiple_of(a * AREA + q * BLK + 64, 16)
                big[j, pl.ds(at, 16), :] = extra[u * 16 : u * 16 + 16, :]

            def go(i, _):
                q = turn(me, i)

                @pl.when(i > 0)
                def _():
                    dispatch_copy(j, a, q, me).start()

                @pl.when(i == 0)
                def _():
                    own_copy(j, a).start()

                return 0

            lax.fori_loop(g * BATCH, (g + 1) * BATCH, go, 0)
            return 0

        lax.fori_loop(0, PEERS // BATCH, batch, 0)

    def assemble(aj, wait):
        def one(i, _):
            q = turn(me, i)
            if wait is not None:
                wait(i, q)
            for c in range(4):
                xs[pl.ds(pl.multiple_of(q * 16, 16), 16), c * GRP : (c + 1) * GRP] = recv[
                    aj, pl.ds(pl.multiple_of(q * BLK + 16 * c, 16), 16), :
                ]
            over[pl.ds(pl.multiple_of(q * 16, 16), 16), :] = recv[
                aj, pl.ds(pl.multiple_of(q * BLK + 64, 16), 16), :
            ]
            return 0

        lax.fori_loop(0, PEERS, one, 0)
        moved = dot(perm[...], over[...]).astype(BF)
        for c in range(4):
            xs[512:640, c * GRP : (c + 1) * GRP] = moved[c * 128 : (c + 1) * 128, :]

    def arrive(j, a):
        def wait(i, q):
            @pl.when(i > 0)
            def _():
                dispatch_copy(j, a, q, q).wait_recv()

            @pl.when(i == 0)
            def _():
                own_copy(j, a).wait()

        assemble(2 * j + a, wait)

    def return_copy(j, q, lands):
        return pltpu.make_async_remote_copy(
            src_ref=recv.at[2 * j, block(q)],
            dst_ref=back.at[j, block(lands)],
            send_sem=r_send.at[j, q],
            recv_sem=r_recv.at[j, lands],
            device_id=(b, q),
            device_id_type=MESH,
        )

    def own_return(j):
        return pltpu.make_async_copy(recv.at[2 * j, block(me)], back.at[j, block(me)], l_sem.at[4 + j])

    def forward(j):
        arrive(j, 0)

        def flip(c, _):
            at = pl.ds(pl.multiple_of(c * GRP, GRP), GRP)
            xt[at, :] = xs[:, at].T
            return 0

        lax.fori_loop(0, 4, flip, 0)
        load_in(j).wait()

        def part(n, _):
            at = pl.ds(pl.multiple_of(n * 256, 256), 256)
            g = dot(xs[...], win[:, at])
            u = dot(xs[...], win[:, pl.ds(pl.multiple_of(FF + n * 256, 256), 256)])
            gate[:, at] = g
            up[:, at] = u
            h = (g * jax.nn.sigmoid(g) * u).astype(BF)
            hid[:, at] = h
            ht[at, :] = h.T
            return 0

        lax.fori_loop(0, FF // 256, part, 0)
        if j == 0:
            load_in(1).start()
        load_out(j).wait()

        def produce(c, _):
            made = dot(hid[...], wout[:, pl.ds(pl.multiple_of(c * GRP, GRP), GRP)]).astype(BF)
            for q in range(PEERS):
                recv[2 * j, pl.ds(pl.multiple_of(q * BLK + 16 * c, 16), 16), :] = made[
                    16 * q : 16 * q + 16, :
                ]
            side[pl.ds(pl.multiple_of(c * 128, 128), 128), :] = made[512:640, :]
            return 0

        lax.fori_loop(0, 4, produce, 0)
        moved = dot(perm_t[...], side[...]).astype(BF)
        for q in range(PEERS):
            recv[2 * j, q * BLK + 64 : q * BLK + 80, :] = moved[16 * q : 16 * q + 16, :]

        def go(i, _):
            return_copy(j, turn(me, i), me).start()
            return 0

        lax.fori_loop(1, PEERS, go, 0)
        own_return(j).start()

    def unit_rows(u, p):
        at, n = rows_of(p)
        return pl.ds(pl.multiple_of(u * UROWS + at, 128), n)

    def z_copy(j, k, p):
        side_of = lax.rem(jnp.int32(k), 2) if isinstance(k, int) else lax.rem(k, 2)
        to = jnp.where(side_of == 0, right, left)
        return pltpu.make_async_remote_copy(
            src_ref=big.at[j, unit_rows(k, p)],
            dst_ref=parts.at[j, unit_rows(k, p)],
            send_sem=z_send.at[j, k, p],
            recv_sem=z_recv.at[j, k, p],
            device_id=(to, me),
            device_id_type=MESH,
        )

    def unit_of(u):
        odd = lax.rem(u, 2)
        far = jnp.where(u < 2, 2, jnp.where(u < 6, 1 + 2 * odd, 0))
        half = jnp.where(lax.div(u, 2) == 1, 1 - odd, odd)
        return lax.rem(b + far, 4), half

    def backward(j):
        arrive(j, 1)

        def sent(i, _):
            q = turn(me, i)
            dispatch_copy(j, 0, q, me).wait_send()
            dispatch_copy(j, 1, q, me).wait_send()
            return 0

        lax.fori_loop(1, PEERS, sent, 0)

        def unit_out(u, _):
            o, half = unit_of(u)
            term = dot(
                ht[pl.ds(pl.multiple_of(half * 384, 128), 384), :],
                xs[:, pl.ds(pl.multiple_of(o * GRP, GRP), GRP)],
            )
            big[j, unit_rows(u, 0), :] = term.astype(BF)

            @pl.when(u < 4)
            def _():
                z_copy(j, u, 0).start()

            return 0

        lax.fori_loop(0, 8, unit_out, 0)

        def part(n, _):
            at = pl.ds(pl.multiple_of(n * 256, 256), 256)
            grad = dot(xs[...], wout[at, :], ((1,), (1,)))
            g = gate[:, at]
            s = jax.nn.sigmoid(g)
            gg[:, at] = (grad * up[:, at] * s * (1.0 + g * (1.0 - s))).astype(BF)
            gg[:, pl.ds(pl.multiple_of(FF + n * 256, 256), 256)] = (grad * (g * s)).astype(BF)
            return 0

        lax.fori_loop(0, FF // 256, part, 0)
        if j == 0:
            load_out(1).start()

        def unit_in(i, _):
            p = 1 + lax.div(i, 8)
            u = lax.rem(i, 8)
            o, half = unit_of(u)
            term = dot(
                xt[pl.ds(pl.multiple_of(o * GRP + half * 256, 256), 256), :],
                gg[:, pl.ds(pl.multiple_of((p - 1) * GRP, GRP), GRP)],
            )
            big[j, unit_rows(u, p), :] = term.astype(BF)

            @pl.when(u < 4)
            def _():
                z_copy(j, u, p).start()

            return 0

        lax.fori_loop(0, 24, unit_in, 0)

    def fetch(j, k, p, where):
        n = rows_of(p)[1]
        return pltpu.make_async_copy(
            parts.at[j, unit_rows(k, p)], stage.at[where, pl.ds(0, n)], o_sem.at[where]
        )

    def middle(j, p):
        n = rows_of(p)[1]
        for d in range(2):
            z_copy(j, d, p).wait_recv()
            fetch(j, d, p, d).start()
        for d in range(2):
            fetch(j, d, p, d).wait()
            at = unit_rows(4 + d, p)
            both = big[j, at, :].astype(F32) + stage[d, 0:n, :].astype(F32)
            big[j, at, :] = both.astype(BF)
            z_copy(j, 4 + d, p).start()

    def result_copy(j, h, p):
        at, n = rows_of(p)
        if isinstance(p, int) and p == 0:
            to = gout.at[j, pl.ds(384 * h, 384)]
        else:
            to = gin.at[j, pl.ds(256 * h, 256), pl.ds(pl.multiple_of((p - 1) * GRP, GRP), GRP)]
        return pltpu.make_async_copy(big.at[j, unit_rows(6 + h, p)], to, o_sem.at[4 + h])

    def finish(j, p):
        n = rows_of(p)[1]
        for k in (3, 2, 4, 5):
            z_copy(j, k, p).wait_recv()
            fetch(j, k, p, k - 2).start()
        for h in range(2):
            fetch(j, 4 + h, p, 2 + h).wait()
            fetch(j, 3 - h, p, 1 - h).wait()
            at = unit_rows(6 + h, p)
            whole = (
                big[j, at, :].astype(F32)
                + stage[2 + h, 0:n, :].astype(F32)
                + stage[1 - h, 0:n, :].astype(F32)
            )
            big[j, at, :] = whole.astype(BF)
            result_copy(j, h, p).start()
        for h in range(2):
            result_copy(j, h, p).wait()

    def each(fn, j, lo, hi):
        if lo == 0:
            fn(j, 0)

        def one(p, _):
            fn(j, p)
            return 0

        lax.fori_loop(max(lo, 1), hi, one, 0)

    def combine(j):
        def arrived(i, _):
            q = turn(me, i)
            return_copy(j, q, q).wait_recv()
            return_copy(j, q, q).wait_send()
            return 0

        lax.fori_loop(1, PEERS, arrived, 0)
        own_return(j).wait()
        whole = pltpu.make_async_copy(back.at[j], recv.at[2 * j + 1], l_sem.at[6])
        whole.start()
        whole.wait()
        assemble(2 * j + 1, None)
        mine = slot[j * PEERS : (j + 1) * PEERS, :]
        heavy = wgt[j * PEERS : (j + 1) * PEERS, :]
        for s in range(4):
            slot4[pl.ds(s, PEERS, stride=4), :] = mine
            wgt4[pl.ds(s, PEERS, stride=4), :] = heavy
        sub = iota((PEERS, MAIN, TOK), 1).astype(F32)
        hot = jnp.where(jnp.broadcast_to(mine[:, None, :], (PEERS, MAIN, TOK)) == sub, 1.0, 0.0)
        hot_w = (hot * heavy[:, None, :]).reshape(512, TOK)
        hot = hot.reshape(512, TOK)
        tail = (16 + lax.rem(iota((128, TOK), 0), 4)).astype(F32)
        hot4 = jnp.where(slot4[...] == tail, 1.0, 0.0)
        hot4_w = hot4 * wgt4[...]
        dots = dot(xs[...], cot[...], ((1,), (1,)))
        near = jnp.sum((dots[0:512, :] * hot).reshape(PEERS, MAIN, TOK), axis=1)
        slot4[...] = dots[512:640, :] * hot4
        for s in range(4):
            near = near + slot4[pl.ds(s, PEERS, stride=4), :]
        aff[j * PEERS : (j + 1) * PEERS, :] = near
        mix_t = jnp.concatenate([hot_w.T, hot4_w.T], axis=1).astype(BF)
        for c in range(4):
            at = slice(c * GRP, (c + 1) * GRP)
            made = dot(mix_t, xs[:, at])
            if j == 0:
                macc[:, at] = made
            else:
                mixed[:, at] = (macc[:, at] + made).astype(BF)

    pl.semaphore_wait(barrier, PEERS + 1)
    dispatch(0, 0)
    dispatch(0, 1)
    dispatch(1, 0)
    dispatch(1, 1)
    forward(0)
    backward(0)
    each(middle, 0, 0, 2)
    forward(1)
    each(middle, 0, 2, 4)
    backward(1)
    each(finish, 0, 0, 4)
    each(middle, 1, 0, 4)
    combine(0)
    combine(1)
    found = []
    for k in range(8):
        found.append(
            jnp.sum(jnp.where(ids[k : k + 1, :] == expert, aff[...], 0.0), axis=0, keepdims=True)
        )
    affinity = jnp.concatenate(found, axis=0)
    score[...] = (affinity - jnp.sum(weights * affinity, axis=0, keepdims=True)) / total
    each(finish, 1, 0, 4)

    def sent(j, p):
        for k in range(6):
            z_copy(j, k, p).wait_send()

    each(sent, 0, 0, 4)
    each(sent, 1, 0, 4)


def shards(tokens, expert_ids, gate_scores, w_in, w_out, cotangent):
    vm = pl.BlockSpec(memory_space=pltpu.VMEM)
    anywhere = pl.BlockSpec(memory_space=pl.ANY)
    mixed, score_t, grad_in, grad_out, _, _ = pl.pallas_call(
        kernel,
        out_shape=[
            jax.ShapeDtypeStruct((TOK, D), BF),
            jax.ShapeDtypeStruct((8, TOK), F32),
            jax.ShapeDtypeStruct((2, 512, 2 * FF), BF),
            jax.ShapeDtypeStruct((2, FF, 512), BF),
            jax.ShapeDtypeStruct((2, AREA, GRP), BF),
            jax.ShapeDtypeStruct((2, 6 * UROWS, GRP), BF),
        ],
        in_specs=[vm, vm, vm, vm, anywhere, anywhere],
        out_specs=[vm, vm, anywhere, anywhere, anywhere, anywhere],
        scratch_shapes=[
            pltpu.VMEM((2, 8 * UROWS, GRP), BF),
            pltpu.VMEM((4, AREA, GRP), BF),
            pltpu.VMEM((D, 2 * FF), BF),
            pltpu.VMEM((FF, D), BF),
            pltpu.VMEM((ROWS, D), BF),
            pltpu.VMEM((D, ROWS), BF),
            pltpu.VMEM((FF, ROWS), BF),
            pltpu.VMEM((ROWS, FF), BF),
            pltpu.VMEM((ROWS, FF), F32),
            pltpu.VMEM((ROWS, FF), F32),
            pltpu.VMEM((ROWS, 2 * FF), BF),
            pltpu.VMEM((4, 384, GRP), BF),
            pltpu.VMEM((64, TOK), F32),
            pltpu.VMEM((64, TOK), F32),
            pltpu.VMEM((8, TOK), F32),
            pltpu.VMEM((GRP, GRP), BF),
            pltpu.VMEM((GRP, GRP), BF),
            pltpu.VMEM((GRP, GRP), BF),
            pltpu.VMEM((GRP, GRP), BF),
            pltpu.VMEM((128, TOK), F32),
            pltpu.VMEM((128, TOK), F32),
            pltpu.VMEM((64, TOK), F32),
            pltpu.VMEM((TOK, D), F32),
            pltpu.SemaphoreType.DMA((4, PEERS)),
            pltpu.SemaphoreType.DMA((4, PEERS)),
            pltpu.SemaphoreType.DMA((2, PEERS)),
            pltpu.SemaphoreType.DMA((2, PEERS)),
            pltpu.SemaphoreType.DMA((2, 6, 4)),
            pltpu.SemaphoreType.DMA((2, 6, 4)),
            pltpu.SemaphoreType.DMA((7,)),
            pltpu.SemaphoreType.DMA((2,)),
            pltpu.SemaphoreType.DMA((6,)),
        ],
        compiler_params=pltpu.CompilerParams(
            collective_id=0, has_side_effects=True, vmem_limit_bytes=63 * 2**20
        ),
        cost_estimate=pl.CostEstimate(
            flops=28_000_000_000, bytes_accessed=60_000_000, transcendentals=2_000_000
        ),
    )(tokens, cotangent, expert_ids.T, gate_scores.T, w_in, w_out)
    return (mixed, score_t.T, grad_in, grad_out)


def solution(mesh):
    in_specs = (
        P(("dp", "expert"), None),
        P(("dp", "expert"), None),
        P(("dp", "expert"), None),
        P("expert", None, None),
        P("expert", None, None),
        P(("dp", "expert"), None),
    )
    out_specs = (
        P(("dp", "expert"), None),
        P(("dp", "expert"), None),
        P("expert", "dp", None),
        P("expert", None, "dp"),
    )
    return jax.shard_map(shards, mesh=mesh, in_specs=in_specs, out_specs=out_specs, check_vma=False)
```

```python
import functools

import jax
import jax.numpy as jnp
from jax import lax
from jax.experimental import pallas as pl
from jax.experimental.pallas import tpu as pltpu
from jax.sharding import PartitionSpec as P

MESH = pl.DeviceIdType.MESH
BF = jnp.bfloat16
F32 = jnp.float32

TOK = 128
D = 2048
FF = 768
PEERS = 32
MAIN = 16
GRP = 512
BLK = 80
ROWS = PEERS * 20
AREA = PEERS * BLK
UROWS = 384 + 3 * 256
BATCH = 16


def dot(a, b, dims=((1,), (0,))):
    return lax.dot_general(a, b, (dims, ((), ())), preferred_element_type=F32)


def peer(me, i):
    c = lax.rem(me, 2)
    x = lax.rem(lax.div(me, 2), 4)
    y = lax.div(me, 8)
    dc = lax.rem(i, 2)
    dx = lax.rem(lax.div(i, 2), 4)
    dy = lax.div(i, 8)
    return lax.rem(y + dy, 4) * 8 + lax.rem(x + dx, 4) * 2 + lax.rem(c + dc, 2)


def chip(me, n, sign):
    k = lax.rem(n * 7, BATCH)
    x = lax.rem(lax.div(me, 2), 4) + 4 + sign * lax.rem(k, 4)
    y = lax.div(me, 8) + 4 + sign * lax.div(k, 4)
    return lax.rem(y, 4) * 4 + lax.rem(x, 4)


def target(me, n, core):
    return 2 * chip(me, n, 1) + core


def source_of(me, i):
    return 2 * chip(me, lax.div(i, 2), -1) + lax.rem(i, 2)


def iota(shape, dim):
    return lax.broadcasted_iota(jnp.int32, shape, dim)


def rows_of(p):
    if isinstance(p, int):
        return (0, 384) if p == 0 else (384 + 256 * (p - 1), 256)
    return (pl.multiple_of(384 + 256 * (p - 1), 128), 256)


def kernel(
    tok, cot, ids, scores, win_hbm, wout_hbm,
    mixed, score, gin, gout, back, parts,
    big, recv, win, wout, xs, xt, ht, hid, gate, up, gg, stage, slot, wgt, cut, perm, perm_t,
    over, side, slot4, wgt4, aff, macc,
    d_send, d_recv, r_send, r_recv, z_send, z_recv, l_sem, w_sem, o_sem,
):
    b = lax.axis_index("dp")
    me = lax.axis_index("expert")
    right = lax.rem(b + 1, 4)
    left = lax.rem(b + 3, 4)

    def load_in(j):
        return pltpu.make_async_copy(win_hbm.at[j], win, w_sem.at[0])

    def load_out(j):
        return pltpu.make_async_copy(wout_hbm.at[j], wout, w_sem.at[1])

    load_in(0).start()
    load_out(0).start()

    barrier = pltpu.get_barrier_semaphore()

    def greet(i, _):
        pl.semaphore_signal(barrier, inc=1, device_id=(b, peer(me, i)), device_id_type=MESH)
        return 0

    lax.fori_loop(1, PEERS, greet, 0)
    pl.semaphore_signal(barrier, inc=1, device_id=(right, me), device_id_type=MESH)
    pl.semaphore_signal(barrier, inc=1, device_id=(left, me), device_id_type=MESH)

    names = ids[...]
    total = jnp.sum(scores[...], axis=0, keepdims=True)
    weights = scores[...] / total
    row = iota((64, TOK), 0)
    expert = 2 * lax.rem(row, PEERS) + lax.div(row, PEERS)
    member = jnp.zeros((64, TOK), F32)
    weight = jnp.zeros((64, TOK), F32)
    for k in range(8):
        hit = names[k : k + 1, :] == expert
        member = member + jnp.where(hit, 1.0, 0.0)
        weight = weight + jnp.where(hit, weights[k : k + 1, :], 0.0)
    earlier = jnp.where(iota((TOK, TOK), 0) < iota((TOK, TOK), 1), 1.0, 0.0).astype(BF)
    slot[...] = jnp.where(member > 0.0, dot(member.astype(BF), earlier), -1.0)
    wgt[...] = weight

    r0, r1 = iota((GRP, GRP), 0), iota((GRP, GRP), 1)

    def place(m):
        r = lax.rem(m, 128)
        return 16 * lax.div(r, 4) + 4 * lax.div(m, 128) + lax.rem(r, 4)

    perm[...] = jnp.where(r1 == place(r0), 1.0, 0.0).astype(BF)
    perm_t[...] = jnp.where(r0 == place(r1), 1.0, 0.0).astype(BF)

    main_slot = iota((MAIN, TOK), 0).astype(F32)
    over_row = iota((MAIN, TOK), 0)
    over_slot = (16 + lax.rem(over_row, 4)).astype(F32)
    group = lax.rem(lax.div(iota((BATCH * MAIN, TOK), 0), 4), 4)

    def block(q):
        return pl.ds(pl.multiple_of(q * BLK, 16), BLK)

    def send_row(a, q):
        return lax.rem(q, 2) * AREA + a * (AREA // 2) + lax.div(q, 2) * BLK

    def send_block(j, a, q):
        return big.at[j, pl.ds(pl.multiple_of(send_row(a, q), 16), BLK)]

    def dispatch_copy(j, a, q, lands):
        return pltpu.make_async_remote_copy(
            src_ref=send_block(j, a, q),
            dst_ref=recv.at[2 * j + a, block(lands)],
            send_sem=d_send.at[2 * j + a, q],
            recv_sem=d_recv.at[2 * j + a, lands],
            device_id=(b, q),
            device_id_type=MESH,
        )

    def own_copy(j, a):
        return pltpu.make_async_copy(
            send_block(j, a, me), recv.at[2 * j + a, block(me)], l_sem.at[2 * j + a]
        )

    def make(j, a, core):
        source = (tok, cot)[a]
        hots, overs, w_main, w_over = [], [], [], []
        for u in range(BATCH):
            q = target(me, u, core)
            mine = slot[pl.ds(j * PEERS + q, 1), :]
            hot = jnp.where(main_slot == mine, 1.0, 0.0)
            hot4 = jnp.where(over_slot == mine, 1.0, 0.0)
            hots.append(hot)
            overs.append(hot4)
            if a == 1:
                heavy = wgt[pl.ds(j * PEERS + q, 1), :]
                w_main.append(jnp.sum(hot * heavy, axis=1, keepdims=True))
                w_over.append(jnp.sum(hot4 * heavy, axis=1, keepdims=True))
        pick = jnp.concatenate(hots, axis=0).astype(BF)
        pick4 = jnp.concatenate(overs, axis=0)
        scale = jnp.concatenate(w_main, axis=0) if a == 1 else None
        scale4 = jnp.concatenate(w_over, axis=0) if a == 1 else None
        extra = None
        for c in range(4):
            columns = source[:, c * GRP : (c + 1) * GRP]
            rows = dot(pick, columns)
            more = dot(jnp.where(group == c, pick4, 0.0).astype(BF), columns)
            extra = more if extra is None else extra + more
            if a == 1:
                rows = rows * scale
            rows = rows.astype(BF)
            for u in range(BATCH):
                at = pl.multiple_of(send_row(a, target(me, u, core)) + 16 * c, 16)
                big[j, pl.ds(at, 16), :] = rows[u * 16 : u * 16 + 16, :]
        if a == 1:
            extra = extra * scale4
        extra = extra.astype(BF)
        for u in range(BATCH):
            at = pl.multiple_of(send_row(a, target(me, u, core)) + 64, 16)
            big[j, pl.ds(at, 16), :] = extra[u * 16 : u * 16 + 16, :]

    def gone(j, a, core):
        def one(n, _):
            q = target(me, n, core)

            @pl.when(q != me)
            def _():
                dispatch_copy(j, a, q, me).wait_send()

            return 0

        lax.fori_loop(0, BATCH, one, 0)

    def launch(j, a, core, after=None):
        def go(n, _):
            q = target(me, n, core)
            if after is not None:
                aj, aa, ac = after
                before = target(me, n, ac)

                @pl.when(before != me)
                def _():
                    dispatch_copy(aj, aa, before, me).wait_send()

            @pl.when(q != me)
            def _():
                dispatch_copy(j, a, q, me).start()

            @pl.when(q == me)
            def _():
                own_copy(j, a).start()

            return 0

        lax.fori_loop(0, BATCH, go, 0)

    def assemble(aj, wait):
        def one(i, _):
            q = source_of(me, i)
            if wait is not None:
                wait(i, q)
            for c in range(4):
                xs[pl.ds(pl.multiple_of(q * 16, 16), 16), c * GRP : (c + 1) * GRP] = recv[
                    aj, pl.ds(pl.multiple_of(q * BLK + 16 * c, 16), 16), :
                ]
            over[pl.ds(pl.multiple_of(q * 16, 16), 16), :] = recv[
                aj, pl.ds(pl.multiple_of(q * BLK + 64, 16), 16), :
            ]
            return 0

        lax.fori_loop(0, PEERS, one, 0)
        moved = dot(perm[...], over[...]).astype(BF)
        for c in range(4):
            xs[512:640, c * GRP : (c + 1) * GRP] = moved[c * 128 : (c + 1) * 128, :]

    def arrive(j, a):
        def wait(i, q):
            @pl.when(q != me)
            def _():
                dispatch_copy(j, a, q, q).wait_recv()

            @pl.when(q == me)
            def _():
                own_copy(j, a).wait()

        assemble(2 * j + a, wait)

    def return_copy(j, q, lands):
        return pltpu.make_async_remote_copy(
            src_ref=recv.at[2 * j, block(q)],
            dst_ref=back.at[j, block(lands)],
            send_sem=r_send.at[j, q],
            recv_sem=r_recv.at[j, lands],
            device_id=(b, q),
            device_id_type=MESH,
        )

    def own_return(j):
        return pltpu.make_async_copy(recv.at[2 * j, block(me)], back.at[j, block(me)], l_sem.at[4 + j])

    def forward(j):
        arrive(j, 0)
        if j == 0:
            pl.when(core == 1)(second)

        def flip(c, _):
            at = pl.ds(pl.multiple_of(c * GRP, GRP), GRP)
            xt[at, :] = xs[:, at].T
            return 0

        lax.fori_loop(0, 4, flip, 0)
        load_in(j).wait()

        def part(n, _):
            at = pl.ds(pl.multiple_of(n * 256, 256), 256)
            g = dot(xs[...], win[:, at])
            u = dot(xs[...], win[:, pl.ds(pl.multiple_of(FF + n * 256, 256), 256)])
            gate[:, at] = g
            up[:, at] = u
            h = (g * jax.nn.sigmoid(g) * u).astype(BF)
            hid[:, at] = h
            ht[at, :] = h.T
            return 0

        lax.fori_loop(0, FF // 256, part, 0)
        if j == 0:
            load_in(1).start()
        load_out(j).wait()

        def produce(c, _):
            made = dot(hid[...], wout[:, pl.ds(pl.multiple_of(c * GRP, GRP), GRP)]).astype(BF)
            for q in range(PEERS):
                recv[2 * j, pl.ds(pl.multiple_of(q * BLK + 16 * c, 16), 16), :] = made[
                    16 * q : 16 * q + 16, :
                ]
            side[pl.ds(pl.multiple_of(c * 128, 128), 128), :] = made[512:640, :]
            return 0

        lax.fori_loop(0, 4, produce, 0)
        moved = dot(perm_t[...], side[...]).astype(BF)
        for q in range(PEERS):
            recv[2 * j, q * BLK + 64 : q * BLK + 80, :] = moved[16 * q : 16 * q + 16, :]

    def send_back(j):
        def go(i, _):
            q = source_of(me, i)

            @pl.when(q != me)
            def _():
                return_copy(j, q, me).start()

            return 0

        lax.fori_loop(0, PEERS, go, 0)
        own_return(j).start()

    def unit_rows(u, p):
        at, n = rows_of(p)
        return pl.ds(pl.multiple_of(u * UROWS + at, 128), n)

    def unit_at(j, u, p):
        at, n = rows_of(p)
        if u < 2:
            buf, row = j, u * UROWS
        elif u < 4:
            buf, row = 1 - j, (2 * AREA if j == 0 else AREA) + (u - 2) * UROWS
        else:
            buf, row = j, 2 * AREA + (u - 4) * UROWS
        return buf, pl.ds(pl.multiple_of(row + at, 128), n)

    def z_copy(j, k, p):
        return pltpu.make_async_remote_copy(
            src_ref=big.at[unit_at(j, k, p)],
            dst_ref=parts.at[j, unit_rows(k, p)],
            send_sem=z_send.at[j, k, p],
            recv_sem=z_recv.at[j, k, p],
            device_id=((right, left)[k % 2], me),
            device_id_type=MESH,
        )

    owners = ((2, 0, 1, (0, 1)), (1, 4, 2, (2,)), (3, 3, 5, (3,)), (0, 6, 7, ()))

    def put(j, p, entry, term):
        n = rows_of(p)[1]
        _, first, second, leave = entry
        for u, piece in ((first, term[0:n, :]), (second, term[n : 2 * n, :])):
            buf, at = unit_at(j, u, p)
            big[buf, at, :] = piece
        for u in leave:
            z_copy(j, u, p).start()

    def backward(j):
        arrive(j, 1)

        if j == 1:
            for a in range(2):
                gone(0, a, 1)
                gone(1, a, 0)
            each(lambda j, p: [z_copy(j, k, p).wait_send() for k in (2, 3)], 0, 0, 4)
        for entry in owners:
            o = lax.rem(b + entry[0], 4)
            put(j, 0, entry, dot(ht[...], xs[:, pl.ds(pl.multiple_of(o * GRP, GRP), GRP)]).astype(BF))

        def part(n, _):
            at = pl.ds(pl.multiple_of(n * 256, 256), 256)
            grad = dot(xs[...], wout[at, :], ((1,), (1,)))
            g = gate[:, at]
            s = jax.nn.sigmoid(g)
            gg[:, at] = (grad * up[:, at] * s * (1.0 + g * (1.0 - s))).astype(BF)
            gg[:, pl.ds(pl.multiple_of(FF + n * 256, 256), 256)] = (grad * (g * s)).astype(BF)
            return 0

        lax.fori_loop(0, FF // 256, part, 0)
        if j == 0:
            load_out(1).start()

        def unit_in(p, _):
            columns = pl.ds(pl.multiple_of((p - 1) * GRP, GRP), GRP)
            for entry in owners:
                o = lax.rem(b + entry[0], 4)
                rows = pl.ds(pl.multiple_of(o * GRP, GRP), GRP)
                put(j, p, entry, dot(xt[rows, :], gg[:, columns]).astype(BF))
            return 0

        lax.fori_loop(1, 4, unit_in, 0)

    def fetch(j, k, p, where):
        n = rows_of(p)[1]
        return pltpu.make_async_copy(
            parts.at[j, unit_rows(k, p)], stage.at[where, pl.ds(0, n)], o_sem.at[where]
        )

    def middle(j, p):
        n = rows_of(p)[1]
        for d in range(2):
            z_copy(j, d, p).wait_recv()
            fetch(j, d, p, d).start()
        for d in range(2):
            fetch(j, d, p, d).wait()
            buf, at = unit_at(j, 4 + d, p)
            both = big[buf, at, :].astype(F32) + stage[d, 0:n, :].astype(F32)
            big[buf, at, :] = both.astype(BF)
            z_copy(j, 4 + d, p).start()

    def result_copy(j, h, p):
        if isinstance(p, int):
            to = gout.at[j, pl.ds(384 * h, 384)]
        else:
            to = gin.at[j, pl.ds(256 * h, 256), pl.ds(pl.multiple_of((p - 1) * GRP, GRP), GRP)]
        return pltpu.make_async_copy(big.at[unit_at(j, 6 + h, p)], to, o_sem.at[4 + h])

    def finish(j, p):
        n = rows_of(p)[1]
        for k in (3, 2, 4, 5):
            z_copy(j, k, p).wait_recv()
            fetch(j, k, p, k - 2).start()
        for h in range(2):
            fetch(j, 4 + h, p, 2 + h).wait()
            fetch(j, 3 - h, p, 1 - h).wait()
            buf, at = unit_at(j, 6 + h, p)
            whole = (
                big[buf, at, :].astype(F32)
                + stage[2 + h, 0:n, :].astype(F32)
                + stage[1 - h, 0:n, :].astype(F32)
            )
            big[buf, at, :] = whole.astype(BF)
            result_copy(j, h, p).start()
        for h in range(2):
            result_copy(j, h, p).wait()

    def each(fn, j, lo, hi):
        if lo == 0:
            fn(j, 0)

        def one(p, _):
            fn(j, p)
            return 0

        lax.fori_loop(max(lo, 1), hi, one, 0)

    def combine(j):
        def arrived(i, _):
            q = peer(me, i)
            return_copy(j, q, q).wait_recv()
            return_copy(j, q, q).wait_send()
            return 0

        lax.fori_loop(1, PEERS, arrived, 0)
        own_return(j).wait()
        whole = pltpu.make_async_copy(back.at[j], recv.at[2 * j + 1], l_sem.at[6])
        whole.start()
        whole.wait()
        assemble(2 * j + 1, None)
        mine = slot[j * PEERS : (j + 1) * PEERS, :]
        heavy = wgt[j * PEERS : (j + 1) * PEERS, :]
        for s in range(4):
            slot4[pl.ds(s, PEERS, stride=4), :] = mine
            wgt4[pl.ds(s, PEERS, stride=4), :] = heavy
        sub = iota((PEERS, MAIN, TOK), 1).astype(F32)
        hot = jnp.where(jnp.broadcast_to(mine[:, None, :], (PEERS, MAIN, TOK)) == sub, 1.0, 0.0)
        hot_w = (hot * heavy[:, None, :]).reshape(512, TOK)
        hot = hot.reshape(512, TOK)
        tail = (16 + lax.rem(iota((128, TOK), 0), 4)).astype(F32)
        hot4 = jnp.where(slot4[...] == tail, 1.0, 0.0)
        hot4_w = hot4 * wgt4[...]
        dots = dot(xs[...], cot[...], ((1,), (1,)))
        near = jnp.sum((dots[0:512, :] * hot).reshape(PEERS, MAIN, TOK), axis=1)
        slot4[...] = dots[512:640, :] * hot4
        for s in range(4):
            near = near + slot4[pl.ds(s, PEERS, stride=4), :]
        aff[j * PEERS : (j + 1) * PEERS, :] = near
        mix_t = jnp.concatenate([hot_w.T, hot4_w.T], axis=1).astype(BF)
        for c in range(4):
            at = slice(c * GRP, (c + 1) * GRP)
            made = dot(mix_t, xs[:, at])
            if j == 0:
                macc[:, at] = made
            else:
                mixed[:, at] = (macc[:, at] + made).astype(BF)

    core = lax.rem(me, 2)

    def first():
        launch(0, 0, 1, (0, 1, 0))
        launch(0, 1, 1)

    def second():
        for target_core in range(2):
            for a in range(2):
                launch(1, a, target_core)

    make(0, 0, 0)
    pl.semaphore_wait(barrier, PEERS + 1)
    launch(0, 0, 0)
    for a, target_core in ((1, 0), (0, 1), (1, 1)):
        make(0, a, target_core)
    launch(0, 1, 0, (0, 0, 0))
    for target_core in range(2):
        for a in range(2):
            make(1, a, target_core)
    pl.when(core == 1)(first)
    forward(0)
    pl.when(core == 0)(first)
    backward(0)
    pl.when(core == 0)(second)
    each(middle, 0, 0, 4)
    forward(1)
    backward(1)
    send_back(0)
    send_back(1)
    each(finish, 0, 0, 4)
    each(middle, 1, 0, 4)
    combine(0)
    combine(1)
    found = []
    for k in range(8):
        found.append(
            jnp.sum(jnp.where(ids[k : k + 1, :] == expert, aff[...], 0.0), axis=0, keepdims=True)
        )
    affinity = jnp.concatenate(found, axis=0)
    score[...] = (affinity - jnp.sum(weights * affinity, axis=0, keepdims=True)) / total

    each(finish, 1, 0, 4)
    for a in range(2):
        gone(1, a, 1)

    def last(j, p):
        for k in range(6):
            if j == 1 or k not in (2, 3):
                z_copy(j, k, p).wait_send()

    each(last, 0, 0, 4)
    each(last, 1, 0, 4)


def shards(tokens, expert_ids, gate_scores, w_in, w_out, cotangent):
    vm = pl.BlockSpec(memory_space=pltpu.VMEM)
    anywhere = pl.BlockSpec(memory_space=pl.ANY)
    mixed, score_t, grad_in, grad_out, _, _ = pl.pallas_call(
        kernel,
        out_shape=[
            jax.ShapeDtypeStruct((TOK, D), BF),
            jax.ShapeDtypeStruct((8, TOK), F32),
            jax.ShapeDtypeStruct((2, 512, 2 * FF), BF),
            jax.ShapeDtypeStruct((2, FF, 512), BF),
            jax.ShapeDtypeStruct((2, AREA, GRP), BF),
            jax.ShapeDtypeStruct((2, 6 * UROWS, GRP), BF),
        ],
        in_specs=[vm, vm, vm, vm, anywhere, anywhere],
        out_specs=[vm, vm, anywhere, anywhere, anywhere, anywhere],
        scratch_shapes=[
            pltpu.VMEM((2, 2 * AREA + 4 * UROWS, GRP), BF),
            pltpu.VMEM((4, AREA, GRP), BF),
            pltpu.VMEM((D, 2 * FF), BF),
            pltpu.VMEM((FF, D), BF),
            pltpu.VMEM((ROWS, D), BF),
            pltpu.VMEM((D, ROWS), BF),
            pltpu.VMEM((FF, ROWS), BF),
            pltpu.VMEM((ROWS, FF), BF),
            pltpu.VMEM((ROWS, FF), F32),
            pltpu.VMEM((ROWS, FF), F32),
            pltpu.VMEM((ROWS, 2 * FF), BF),
            pltpu.VMEM((4, 384, GRP), BF),
            pltpu.VMEM((64, TOK), F32),
            pltpu.VMEM((64, TOK), F32),
            pltpu.VMEM((8, TOK), F32),
            pltpu.VMEM((GRP, GRP), BF),
            pltpu.VMEM((GRP, GRP), BF),
            pltpu.VMEM((GRP, GRP), BF),
            pltpu.VMEM((GRP, GRP), BF),
            pltpu.VMEM((128, TOK), F32),
            pltpu.VMEM((128, TOK), F32),
            pltpu.VMEM((64, TOK), F32),
            pltpu.VMEM((TOK, D), F32),
            pltpu.SemaphoreType.DMA((4, PEERS)),
            pltpu.SemaphoreType.DMA((4, PEERS)),
            pltpu.SemaphoreType.DMA((2, PEERS)),
            pltpu.SemaphoreType.DMA((2, PEERS)),
            pltpu.SemaphoreType.DMA((2, 6, 4)),
            pltpu.SemaphoreType.DMA((2, 6, 4)),
            pltpu.SemaphoreType.DMA((7,)),
            pltpu.SemaphoreType.DMA((2,)),
            pltpu.SemaphoreType.DMA((6,)),
        ],
        compiler_params=pltpu.CompilerParams(
            collective_id=0, has_side_effects=True, vmem_limit_bytes=63 * 2**20
        ),
        cost_estimate=pl.CostEstimate(
            flops=28_000_000_000, bytes_accessed=60_000_000, transcendentals=2_000_000
        ),
    )(tokens, cotangent, expert_ids.T, gate_scores.T, w_in, w_out)
    return (mixed, score_t.T, grad_in, grad_out)


def solution(mesh):
    in_specs = (
        P(("dp", "expert"), None),
        P(("dp", "expert"), None),
        P(("dp", "expert"), None),
        P("expert", None, None),
        P("expert", None, None),
        P(("dp", "expert"), None),
    )
    out_specs = (
        P(("dp", "expert"), None),
        P(("dp", "expert"), None),
        P("expert", "dp", None),
        P("expert", None, "dp"),
    )
    return jax.shard_map(shards, mesh=mesh, in_specs=in_specs, out_specs=out_specs, check_vma=False)
```

```python
import functools

import jax
import jax.numpy as jnp
from jax import lax
from jax.experimental import pallas as pl
from jax.experimental.pallas import tpu as pltpu
from jax.sharding import PartitionSpec as P

MESH = pl.DeviceIdType.MESH
BF = jnp.bfloat16
F32 = jnp.float32

TOK = 128
D = 2048
FF = 768
PEERS = 32
MAIN = 16
GRP = 512
BLK = 80
ROWS = PEERS * 20
AREA = PEERS * BLK
UROWS = 384 + 3 * 256
BATCH = 16


def dot(a, b, dims=((1,), (0,))):
    return lax.dot_general(a, b, (dims, ((), ())), preferred_element_type=F32)


def peer(me, i):
    c = lax.rem(me, 2)
    x = lax.rem(lax.div(me, 2), 4)
    y = lax.div(me, 8)
    dc = lax.rem(i, 2)
    dx = lax.rem(lax.div(i, 2), 4)
    dy = lax.div(i, 8)
    return lax.rem(y + dy, 4) * 8 + lax.rem(x + dx, 4) * 2 + lax.rem(c + dc, 2)


def chip(me, n, sign):
    k = lax.rem(n * 7, BATCH)
    x = lax.rem(lax.div(me, 2), 4) + 4 + sign * lax.rem(k, 4)
    y = lax.div(me, 8) + 4 + sign * lax.div(k, 4)
    return lax.rem(y, 4) * 4 + lax.rem(x, 4)


def target(me, n, core):
    return 2 * chip(me, n, 1) + core


def source_of(me, i):
    return 2 * chip(me, lax.div(i, 2), -1) + lax.rem(i, 2)


def iota(shape, dim):
    return lax.broadcasted_iota(jnp.int32, shape, dim)


def rows_of(p):
    if isinstance(p, int):
        return (0, 384) if p == 0 else (384 + 256 * (p - 1), 256)
    return (pl.multiple_of(384 + 256 * (p - 1), 128), 256)


def kernel(
    tok, cot, ids, scores, win_hbm, wout_hbm,
    mixed, score, gin, gout, back, parts,
    big, recv, win, wout, xs, xt, ht, hid, gate, up, gg, stage, slot, wgt, cut, perm, perm_t,
    over, side, slot4, wgt4, aff, macc,
    d_send, d_recv, r_send, r_recv, z_send, z_recv, l_sem, w_sem, o_sem, g_sem, b_sem,
):
    b = lax.axis_index("dp")
    me = lax.axis_index("expert")
    right = lax.rem(b + 1, 4)
    left = lax.rem(b + 3, 4)

    def load_in(j):
        return pltpu.make_async_copy(win_hbm.at[j], win, w_sem.at[0])

    def load_out(j):
        return pltpu.make_async_copy(wout_hbm.at[j], wout, w_sem.at[1])

    load_in(0).start()
    load_out(0).start()

    barrier = pltpu.get_barrier_semaphore()

    def greet(i, _):
        pl.semaphore_signal(barrier, inc=1, device_id=(b, peer(me, i)), device_id_type=MESH)
        return 0

    lax.fori_loop(1, PEERS, greet, 0)
    pl.semaphore_signal(barrier, inc=1, device_id=(right, me), device_id_type=MESH)
    pl.semaphore_signal(barrier, inc=1, device_id=(left, me), device_id_type=MESH)

    names = ids[...]
    total = jnp.sum(scores[...], axis=0, keepdims=True)
    weights = scores[...] / total
    row = iota((64, TOK), 0)
    expert = 2 * lax.rem(row, PEERS) + lax.div(row, PEERS)
    member = jnp.zeros((64, TOK), F32)
    weight = jnp.zeros((64, TOK), F32)
    for k in range(8):
        hit = names[k : k + 1, :] == expert
        member = member + jnp.where(hit, 1.0, 0.0)
        weight = weight + jnp.where(hit, weights[k : k + 1, :], 0.0)
    earlier = jnp.where(iota((TOK, TOK), 0) < iota((TOK, TOK), 1), 1.0, 0.0).astype(BF)
    slot[...] = jnp.where(member > 0.0, dot(member.astype(BF), earlier), -1.0)
    wgt[...] = weight

    r0, r1 = iota((GRP, GRP), 0), iota((GRP, GRP), 1)

    def place(m):
        r = lax.rem(m, 128)
        return 16 * lax.div(r, 4) + 4 * lax.div(m, 128) + lax.rem(r, 4)

    perm[...] = jnp.where(r1 == place(r0), 1.0, 0.0).astype(BF)
    perm_t[...] = jnp.where(r0 == place(r1), 1.0, 0.0).astype(BF)

    main_slot = iota((MAIN, TOK), 0).astype(F32)
    over_row = iota((MAIN, TOK), 0)
    over_slot = (16 + lax.rem(over_row, 4)).astype(F32)
    group = lax.rem(lax.div(iota((BATCH * MAIN, TOK), 0), 4), 4)

    def block(q):
        return pl.ds(pl.multiple_of(q * BLK, 16), BLK)

    def send_row(a, q):
        return lax.rem(q, 2) * AREA + a * (AREA // 2) + lax.div(q, 2) * BLK

    def send_block(j, a, q):
        return big.at[j, pl.ds(pl.multiple_of(send_row(a, q), 16), BLK)]

    def dispatch_copy(j, a, q, lands):
        return pltpu.make_async_remote_copy(
            src_ref=send_block(j, a, q),
            dst_ref=recv.at[2 * j + a, block(lands)],
            send_sem=d_send.at[2 * j + a, q],
            recv_sem=d_recv.at[2 * j + a, lands],
            device_id=(b, q),
            device_id_type=MESH,
        )

    def own_copy(j, a):
        return pltpu.make_async_copy(
            send_block(j, a, me), recv.at[2 * j + a, block(me)], l_sem.at[2 * j + a]
        )

    def make(j, a, core):
        source = (tok, cot)[a]
        hots, overs, w_main, w_over = [], [], [], []
        for u in range(BATCH):
            q = target(me, u, core)
            mine = slot[pl.ds(j * PEERS + q, 1), :]
            hot = jnp.where(main_slot == mine, 1.0, 0.0)
            hot4 = jnp.where(over_slot == mine, 1.0, 0.0)
            hots.append(hot)
            overs.append(hot4)
            if a == 1:
                heavy = wgt[pl.ds(j * PEERS + q, 1), :]
                w_main.append(jnp.sum(hot * heavy, axis=1, keepdims=True))
                w_over.append(jnp.sum(hot4 * heavy, axis=1, keepdims=True))
        pick = jnp.concatenate(hots, axis=0).astype(BF)
        pick4 = jnp.concatenate(overs, axis=0)
        scale = jnp.concatenate(w_main, axis=0) if a == 1 else None
        scale4 = jnp.concatenate(w_over, axis=0) if a == 1 else None
        extra = None
        for c in range(4):
            columns = source[:, c * GRP : (c + 1) * GRP]
            rows = dot(pick, columns)
            more = dot(jnp.where(group == c, pick4, 0.0).astype(BF), columns)
            extra = more if extra is None else extra + more
            if a == 1:
                rows = rows * scale
            rows = rows.astype(BF)
            for u in range(BATCH):
                at = pl.multiple_of(send_row(a, target(me, u, core)) + 16 * c, 16)
                big[j, pl.ds(at, 16), :] = rows[u * 16 : u * 16 + 16, :]
        if a == 1:
            extra = extra * scale4
        extra = extra.astype(BF)
        for u in range(BATCH):
            at = pl.multiple_of(send_row(a, target(me, u, core)) + 64, 16)
            big[j, pl.ds(at, 16), :] = extra[u * 16 : u * 16 + 16, :]

    def gone(j, a, core):
        def one(n, _):
            q = target(me, n, core)

            @pl.when(q != me)
            def _():
                dispatch_copy(j, a, q, me).wait_send()

            return 0

        lax.fori_loop(0, BATCH, one, 0)

    def launch(j, a, core, after=None):
        def go(n, _):
            q = target(me, n, core)
            if after is not None:
                aj, aa, ac = after
                before = target(me, n, ac)

                @pl.when(before != me)
                def _():
                    dispatch_copy(aj, aa, before, me).wait_send()

            @pl.when(q != me)
            def _():
                dispatch_copy(j, a, q, me).start()

            @pl.when(q == me)
            def _():
                own_copy(j, a).start()

            return 0

        lax.fori_loop(0, BATCH, go, 0)

    def assemble(aj, wait):
        def one(i, _):
            q = source_of(me, i)
            if wait is not None:
                wait(i, q)
            for c in range(4):
                xs[pl.ds(pl.multiple_of(q * 16, 16), 16), c * GRP : (c + 1) * GRP] = recv[
                    aj, pl.ds(pl.multiple_of(q * BLK + 16 * c, 16), 16), :
                ]
            over[pl.ds(pl.multiple_of(q * 16, 16), 16), :] = recv[
                aj, pl.ds(pl.multiple_of(q * BLK + 64, 16), 16), :
            ]
            return 0

        lax.fori_loop(0, PEERS, one, 0)
        moved = dot(perm[...], over[...]).astype(BF)
        for c in range(4):
            xs[512:640, c * GRP : (c + 1) * GRP] = moved[c * 128 : (c + 1) * 128, :]

    def arrive(j, a):
        def wait(i, q):
            @pl.when(q != me)
            def _():
                dispatch_copy(j, a, q, q).wait_recv()

            @pl.when(q == me)
            def _():
                own_copy(j, a).wait()

        assemble(2 * j + a, wait)

    def return_copy(j, q, lands):
        return pltpu.make_async_remote_copy(
            src_ref=recv.at[2 * j, block(q)],
            dst_ref=back.at[j, block(lands)],
            send_sem=r_send.at[j, q],
            recv_sem=r_recv.at[j, lands],
            device_id=(b, q),
            device_id_type=MESH,
        )

    def own_return(j):
        return pltpu.make_async_copy(recv.at[2 * j, block(me)], back.at[j, block(me)], l_sem.at[4 + j])

    def forward(j):
        arrive(j, 0)
        if j == 0:
            pl.when(core == 1)(second)

        def flip(c, _):
            at = pl.ds(pl.multiple_of(c * GRP, GRP), GRP)
            xt[at, :] = xs[:, at].T
            return 0

        lax.fori_loop(0, 4, flip, 0)
        load_in(j).wait()

        def part(n, _):
            at = pl.ds(pl.multiple_of(n * 256, 256), 256)
            g = dot(xs[...], win[:, at])
            u = dot(xs[...], win[:, pl.ds(pl.multiple_of(FF + n * 256, 256), 256)])
            gate[:, at] = g
            up[:, at] = u
            h = (g * jax.nn.sigmoid(g) * u).astype(BF)
            hid[:, at] = h
            ht[at, :] = h.T
            return 0

        lax.fori_loop(0, FF // 256, part, 0)
        if j == 0:
            load_in(1).start()
        load_out(j).wait()

        def produce(c, _):
            made = dot(hid[...], wout[:, pl.ds(pl.multiple_of(c * GRP, GRP), GRP)]).astype(BF)
            for q in range(PEERS):
                recv[2 * j, pl.ds(pl.multiple_of(q * BLK + 16 * c, 16), 16), :] = made[
                    16 * q : 16 * q + 16, :
                ]
            side[pl.ds(pl.multiple_of(c * 128, 128), 128), :] = made[512:640, :]
            return 0

        lax.fori_loop(0, 4, produce, 0)
        moved = dot(perm_t[...], side[...]).astype(BF)
        for q in range(PEERS):
            recv[2 * j, q * BLK + 64 : q * BLK + 80, :] = moved[16 * q : 16 * q + 16, :]

    def send_back(j):
        def go(i, _):
            q = source_of(me, i)

            @pl.when(q != me)
            def _():
                return_copy(j, q, me).start()

            return 0

        lax.fori_loop(0, PEERS, go, 0)
        own_return(j).start()

    def unit_rows(u, p):
        at, n = rows_of(p)
        return pl.ds(pl.multiple_of(u * UROWS + at, 128), n)

    def unit_at(j, u, p):
        at, n = rows_of(p)
        if u < 2:
            buf, row = j, u * UROWS
        elif u < 4:
            buf, row = 1 - j, (2 * AREA if j == 0 else AREA) + (u - 2) * UROWS
        else:
            buf, row = j, 2 * AREA + (u - 4) * UROWS
        return buf, pl.ds(pl.multiple_of(row + at, 128), n)

    def z_copy(j, k, p):
        return pltpu.make_async_remote_copy(
            src_ref=big.at[unit_at(j, k, p)],
            dst_ref=parts.at[j, unit_rows(k, p)],
            send_sem=z_send.at[j, k, p],
            recv_sem=z_recv.at[j, k, p],
            device_id=((right, left)[k % 2], me),
            device_id_type=MESH,
        )

    owners = ((2, 0, 1, (0, 1)), (1, 4, 2, (2,)), (3, 3, 5, (3,)), (0, 6, 7, ()))

    def put(j, p, entry, term):
        n = rows_of(p)[1]
        _, first, second, leave = entry
        for u, piece in ((first, term[0:n, :]), (second, term[n : 2 * n, :])):
            buf, at = unit_at(j, u, p)
            big[buf, at, :] = piece
        for u in leave:
            z_copy(j, u, p).start()

    def backward(j):
        arrive(j, 1)

        if j == 1:
            for a in range(2):
                gone(0, a, 1)
                gone(1, a, 0)
            each(lambda j, p: [z_copy(j, k, p).wait_send() for k in (2, 3)], 0, 0, 4)
        for entry in owners:
            o = lax.rem(b + entry[0], 4)
            put(j, 0, entry, dot(ht[...], xs[:, pl.ds(pl.multiple_of(o * GRP, GRP), GRP)]).astype(BF))

        def part(n, _):
            at = pl.ds(pl.multiple_of(n * 256, 256), 256)
            grad = dot(xs[...], wout[at, :], ((1,), (1,)))
            g = gate[:, at]
            s = jax.nn.sigmoid(g)
            gg[:, at] = (grad * up[:, at] * s * (1.0 + g * (1.0 - s))).astype(BF)
            gg[:, pl.ds(pl.multiple_of(FF + n * 256, 256), 256)] = (grad * (g * s)).astype(BF)
            return 0

        lax.fori_loop(0, FF // 256, part, 0)
        if j == 0:
            load_out(1).start()

        def unit_in(p, _):
            columns = pl.ds(pl.multiple_of((p - 1) * GRP, GRP), GRP)
            for entry in owners:
                o = lax.rem(b + entry[0], 4)
                rows = pl.ds(pl.multiple_of(o * GRP, GRP), GRP)
                put(j, p, entry, dot(xt[rows, :], gg[:, columns]).astype(BF))
            return 0

        lax.fori_loop(1, 4, unit_in, 0)

    def fetch(j, k, p, where):
        n = rows_of(p)[1]
        return pltpu.make_async_copy(
            parts.at[j, unit_rows(k, p)], stage.at[where, pl.ds(0, n)], o_sem.at[where]
        )

    def middle(j, p):
        n = rows_of(p)[1]
        for d in range(2):
            z_copy(j, d, p).wait_recv()
            fetch(j, d, p, d).start()
        for d in range(2):
            fetch(j, d, p, d).wait()
            buf, at = unit_at(j, 4 + d, p)
            both = big[buf, at, :].astype(F32) + stage[d, 0:n, :].astype(F32)
            big[buf, at, :] = both.astype(BF)
            z_copy(j, 4 + d, p).start()

    def early(j, p):
        n = rows_of(p)[1]
        for k in (3, 2):
            z_copy(j, k, p).wait_recv()
            fetch(j, k, p, k).start()
        for h in range(2):
            fetch(j, 3 - h, p, 3 - h).wait()
            buf, at = unit_at(j, 6 + h, p)
            both = big[buf, at, :].astype(F32) + stage[3 - h, 0:n, :].astype(F32)
            big[buf, at, :] = both.astype(BF)

    def result_copy(j, h, p):
        if isinstance(p, int):
            to = gout.at[j, pl.ds(384 * h, 384)]
        else:
            to = gin.at[j, pl.ds(256 * h, 256), pl.ds(pl.multiple_of((p - 1) * GRP, GRP), GRP)]
        return pltpu.make_async_copy(big.at[unit_at(j, 6 + h, p)], to, g_sem.at[j, h, p])

    def finish(j, p):
        n = rows_of(p)[1]
        for h in range(2):
            z_copy(j, 4 + h, p).wait_recv()
            fetch(j, 4 + h, p, h).start()
        for h in range(2):
            fetch(j, 4 + h, p, h).wait()
            buf, at = unit_at(j, 6 + h, p)
            whole = big[buf, at, :].astype(F32) + stage[h, 0:n, :].astype(F32)
            big[buf, at, :] = whole.astype(BF)
            result_copy(j, h, p).start()

    def each(fn, j, lo, hi):
        if lo == 0:
            fn(j, 0)

        def one(p, _):
            fn(j, p)
            return 0

        lax.fori_loop(max(lo, 1), hi, one, 0)

    def combine(j):
        def take(q):
            return pltpu.make_async_copy(
                back.at[j, block(q)], recv.at[2 * j + 1, block(q)], b_sem.at[q]
            )

        own_return(j).wait()
        take(me).start()

        def arrived(i, _):
            q = peer(me, i)
            return_copy(j, q, q).wait_recv()
            take(q).start()
            return 0

        lax.fori_loop(1, PEERS, arrived, 0)
        assemble(2 * j + 1, lambda i, q: take(q).wait())
        mine = slot[j * PEERS : (j + 1) * PEERS, :]
        heavy = wgt[j * PEERS : (j + 1) * PEERS, :]
        for s in range(4):
            slot4[pl.ds(s, PEERS, stride=4), :] = mine
            wgt4[pl.ds(s, PEERS, stride=4), :] = heavy
        sub = iota((PEERS, MAIN, TOK), 1).astype(F32)
        hot = jnp.where(jnp.broadcast_to(mine[:, None, :], (PEERS, MAIN, TOK)) == sub, 1.0, 0.0)
        hot_w = (hot * heavy[:, None, :]).reshape(512, TOK)
        hot = hot.reshape(512, TOK)
        tail = (16 + lax.rem(iota((128, TOK), 0), 4)).astype(F32)
        hot4 = jnp.where(slot4[...] == tail, 1.0, 0.0)
        hot4_w = hot4 * wgt4[...]
        dots = dot(xs[...], cot[...], ((1,), (1,)))
        near = jnp.sum((dots[0:512, :] * hot).reshape(PEERS, MAIN, TOK), axis=1)
        slot4[...] = dots[512:640, :] * hot4
        for s in range(4):
            near = near + slot4[pl.ds(s, PEERS, stride=4), :]
        aff[j * PEERS : (j + 1) * PEERS, :] = near
        mix_t = jnp.concatenate([hot_w.T, hot4_w.T], axis=1).astype(BF)
        for c in range(4):
            at = slice(c * GRP, (c + 1) * GRP)
            made = dot(mix_t, xs[:, at])
            if j == 0:
                macc[:, at] = made
            else:
                mixed[:, at] = (macc[:, at] + made).astype(BF)

    core = lax.rem(me, 2)

    def first():
        launch(0, 0, 1, (0, 1, 0))
        launch(0, 1, 1)

    def second():
        for target_core in range(2):
            for a in range(2):
                launch(1, a, target_core)

    make(0, 0, 0)
    pl.semaphore_wait(barrier, PEERS + 1)
    launch(0, 0, 0)
    for a, target_core in ((1, 0), (0, 1), (1, 1)):
        make(0, a, target_core)
    launch(0, 1, 0, (0, 0, 0))
    for target_core in range(2):
        for a in range(2):
            make(1, a, target_core)
    pl.when(core == 1)(first)
    forward(0)
    pl.when(core == 0)(first)
    backward(0)
    pl.when(core == 0)(second)
    each(middle, 0, 0, 4)
    forward(1)
    backward(1)
    send_back(0)
    send_back(1)

    def between(j, p):
        middle(1, p)
        early(0, p)
        finish(0, p)

    each(between, 0, 0, 4)
    each(early, 1, 0, 4)
    combine(0)
    each(finish, 1, 0, 2)
    combine(1)
    found = []
    for k in range(8):
        found.append(
            jnp.sum(jnp.where(ids[k : k + 1, :] == expert, aff[...], 0.0), axis=0, keepdims=True)
        )
    affinity = jnp.concatenate(found, axis=0)
    score[...] = (affinity - jnp.sum(weights * affinity, axis=0, keepdims=True)) / total

    each(finish, 1, 2, 4)
    for a in range(2):
        gone(1, a, 1)

    def returned(i, _):
        q = peer(me, i)
        for j in range(2):
            return_copy(j, q, q).wait_send()
        return 0

    lax.fori_loop(1, PEERS, returned, 0)

    def last(j, p):
        for k in range(6):
            if j == 1 or k not in (2, 3):
                z_copy(j, k, p).wait_send()
        for h in range(2):
            result_copy(j, h, p).wait()

    each(last, 0, 0, 4)
    each(last, 1, 0, 4)


def shards(tokens, expert_ids, gate_scores, w_in, w_out, cotangent):
    vm = pl.BlockSpec(memory_space=pltpu.VMEM)
    anywhere = pl.BlockSpec(memory_space=pl.ANY)
    mixed, score_t, grad_in, grad_out, _, _ = pl.pallas_call(
        kernel,
        out_shape=[
            jax.ShapeDtypeStruct((TOK, D), BF),
            jax.ShapeDtypeStruct((8, TOK), F32),
            jax.ShapeDtypeStruct((2, 512, 2 * FF), BF),
            jax.ShapeDtypeStruct((2, FF, 512), BF),
            jax.ShapeDtypeStruct((2, AREA, GRP), BF),
            jax.ShapeDtypeStruct((2, 6 * UROWS, GRP), BF),
        ],
        in_specs=[vm, vm, vm, vm, anywhere, anywhere],
        out_specs=[vm, vm, anywhere, anywhere, anywhere, anywhere],
        scratch_shapes=[
            pltpu.VMEM((2, 2 * AREA + 4 * UROWS, GRP), BF),
            pltpu.VMEM((4, AREA, GRP), BF),
            pltpu.VMEM((D, 2 * FF), BF),
            pltpu.VMEM((FF, D), BF),
            pltpu.VMEM((ROWS, D), BF),
            pltpu.VMEM((D, ROWS), BF),
            pltpu.VMEM((FF, ROWS), BF),
            pltpu.VMEM((ROWS, FF), BF),
            pltpu.VMEM((ROWS, FF), F32),
            pltpu.VMEM((ROWS, FF), F32),
            pltpu.VMEM((ROWS, 2 * FF), BF),
            pltpu.VMEM((4, 384, GRP), BF),
            pltpu.VMEM((64, TOK), F32),
            pltpu.VMEM((64, TOK), F32),
            pltpu.VMEM((8, TOK), F32),
            pltpu.VMEM((GRP, GRP), BF),
            pltpu.VMEM((GRP, GRP), BF),
            pltpu.VMEM((GRP, GRP), BF),
            pltpu.VMEM((GRP, GRP), BF),
            pltpu.VMEM((128, TOK), F32),
            pltpu.VMEM((128, TOK), F32),
            pltpu.VMEM((64, TOK), F32),
            pltpu.VMEM((TOK, D), F32),
            pltpu.SemaphoreType.DMA((4, PEERS)),
            pltpu.SemaphoreType.DMA((4, PEERS)),
            pltpu.SemaphoreType.DMA((2, PEERS)),
            pltpu.SemaphoreType.DMA((2, PEERS)),
            pltpu.SemaphoreType.DMA((2, 6, 4)),
            pltpu.SemaphoreType.DMA((2, 6, 4)),
            pltpu.SemaphoreType.DMA((7,)),
            pltpu.SemaphoreType.DMA((2,)),
            pltpu.SemaphoreType.DMA((4,)),
            pltpu.SemaphoreType.DMA((2, 2, 4)),
            pltpu.SemaphoreType.DMA((PEERS,)),
        ],
        compiler_params=pltpu.CompilerParams(
            collective_id=0, has_side_effects=True, vmem_limit_bytes=63 * 2**20
        ),
        cost_estimate=pl.CostEstimate(
            flops=28_000_000_000, bytes_accessed=60_000_000, transcendentals=2_000_000
        ),
    )(tokens, cotangent, expert_ids.T, gate_scores.T, w_in, w_out)
    return (mixed, score_t.T, grad_in, grad_out)


def solution(mesh):
    in_specs = (
        P(("dp", "expert"), None),
        P(("dp", "expert"), None),
        P(("dp", "expert"), None),
        P("expert", None, None),
        P("expert", None, None),
        P(("dp", "expert"), None),
    )
    out_specs = (
        P(("dp", "expert"), None),
        P(("dp", "expert"), None),
        P("expert", "dp", None),
        P("expert", None, "dp"),
    )
    return jax.shard_map(shards, mesh=mesh, in_specs=in_specs, out_specs=out_specs, check_vma=False)
```

```python
import functools

import jax
import jax.numpy as jnp
from jax import lax
from jax.experimental import pallas as pl
from jax.experimental.pallas import tpu as pltpu
from jax.sharding import PartitionSpec as P

MESH = pl.DeviceIdType.MESH
BF = jnp.bfloat16
F32 = jnp.float32

TOK = 128
D = 2048
FF = 768
PEERS = 32
MAIN = 16
GRP = 512
BLK = 80
ROWS = PEERS * 20
AREA = PEERS * BLK
UROWS = 384 + 3 * 256
BATCH = 16


def dot(a, b, dims=((1,), (0,))):
    return lax.dot_general(a, b, (dims, ((), ())), preferred_element_type=F32)


def peer(me, i):
    c = lax.rem(me, 2)
    x = lax.rem(lax.div(me, 2), 4)
    y = lax.div(me, 8)
    dc = lax.rem(i, 2)
    dx = lax.rem(lax.div(i, 2), 4)
    dy = lax.div(i, 8)
    return lax.rem(y + dy, 4) * 8 + lax.rem(x + dx, 4) * 2 + lax.rem(c + dc, 2)


def chip(me, n, sign):
    k = lax.rem(n * 7, BATCH)
    x = lax.rem(lax.div(me, 2), 4) + 4 + sign * lax.rem(k, 4)
    y = lax.div(me, 8) + 4 + sign * lax.div(k, 4)
    return lax.rem(y, 4) * 4 + lax.rem(x, 4)


def target(me, n, core):
    return 2 * chip(me, n, 1) + core


def source_of(me, i):
    return 2 * chip(me, lax.div(i, 2), -1) + lax.rem(i, 2)


def iota(shape, dim):
    return lax.broadcasted_iota(jnp.int32, shape, dim)


def rows_of(p):
    if isinstance(p, int):
        return (0, 384) if p == 0 else (384 + 256 * (p - 1), 256)
    return (pl.multiple_of(384 + 256 * (p - 1), 128), 256)


def kernel(
    tok, cot, ids, scores, win_hbm, wout_hbm,
    mixed, score, gin, gout, back, parts,
    big, recv, win, wout, xs, xt, ht, hid, gate, up, gg, stage, slot, wgt, cut, perm, perm_t,
    over, side, slot4, wgt4, aff, macc,
    d_send, d_recv, r_send, r_recv, z_send, z_recv, l_sem, w_sem, o_sem, g_sem, b_sem,
):
    b = lax.axis_index("dp")
    me = lax.axis_index("expert")
    right = lax.rem(b + 1, 4)
    left = lax.rem(b + 3, 4)

    def load_in(j):
        return pltpu.make_async_copy(win_hbm.at[j], win, w_sem.at[0])

    def load_out(j):
        return pltpu.make_async_copy(wout_hbm.at[j], wout, w_sem.at[1])

    load_in(0).start()
    load_out(0).start()

    barrier = pltpu.get_barrier_semaphore()

    def greet(i, _):
        pl.semaphore_signal(barrier, inc=1, device_id=(b, peer(me, i)), device_id_type=MESH)
        return 0

    lax.fori_loop(1, PEERS, greet, 0)
    pl.semaphore_signal(barrier, inc=1, device_id=(right, me), device_id_type=MESH)
    pl.semaphore_signal(barrier, inc=1, device_id=(left, me), device_id_type=MESH)

    names = ids[...]
    total = jnp.sum(scores[...], axis=0, keepdims=True)
    weights = scores[...] / total
    row = iota((64, TOK), 0)
    expert = 2 * lax.rem(row, PEERS) + lax.div(row, PEERS)
    member = jnp.zeros((64, TOK), F32)
    weight = jnp.zeros((64, TOK), F32)
    for k in range(8):
        hit = names[k : k + 1, :] == expert
        member = member + jnp.where(hit, 1.0, 0.0)
        weight = weight + jnp.where(hit, weights[k : k + 1, :], 0.0)
    earlier = jnp.where(iota((TOK, TOK), 0) < iota((TOK, TOK), 1), 1.0, 0.0).astype(BF)
    slot[...] = jnp.where(member > 0.0, dot(member.astype(BF), earlier), -1.0)
    wgt[...] = weight

    main_slot = iota((MAIN, TOK), 0).astype(F32)
    over_row = iota((MAIN, TOK), 0)
    over_slot = (16 + lax.rem(over_row, 4)).astype(F32)
    group = lax.rem(lax.div(iota((BATCH * MAIN, TOK), 0), 4), 4)

    def block(q):
        return pl.ds(pl.multiple_of(q * BLK, 16), BLK)

    def send_row(a, q):
        return lax.rem(q, 2) * AREA + a * (AREA // 2) + lax.div(q, 2) * BLK

    def send_block(j, a, q):
        return big.at[j, pl.ds(pl.multiple_of(send_row(a, q), 16), BLK)]

    def dispatch_copy(j, a, q, lands):
        return pltpu.make_async_remote_copy(
            src_ref=send_block(j, a, q),
            dst_ref=recv.at[2 * j + a, block(lands)],
            send_sem=d_send.at[2 * j + a, q],
            recv_sem=d_recv.at[2 * j + a, lands],
            device_id=(b, q),
            device_id_type=MESH,
        )

    def own_copy(j, a):
        return pltpu.make_async_copy(
            send_block(j, a, me), recv.at[2 * j + a, block(me)], l_sem.at[2 * j + a]
        )

    def make(j, a, core):
        source = (tok, cot)[a]
        hots, overs, w_main, w_over = [], [], [], []
        for u in range(BATCH):
            q = target(me, u, core)
            mine = slot[pl.ds(j * PEERS + q, 1), :]
            hot = jnp.where(main_slot == mine, 1.0, 0.0)
            hot4 = jnp.where(over_slot == mine, 1.0, 0.0)
            hots.append(hot)
            overs.append(hot4)
            if a == 1:
                heavy = wgt[pl.ds(j * PEERS + q, 1), :]
                w_main.append(jnp.sum(hot * heavy, axis=1, keepdims=True))
                w_over.append(jnp.sum(hot4 * heavy, axis=1, keepdims=True))
        pick = jnp.concatenate(hots, axis=0).astype(BF)
        pick4 = jnp.concatenate(overs, axis=0)
        scale = jnp.concatenate(w_main, axis=0) if a == 1 else None
        scale4 = jnp.concatenate(w_over, axis=0) if a == 1 else None
        extra = None
        for c in range(4):
            columns = source[:, c * GRP : (c + 1) * GRP]
            rows = dot(pick, columns)
            more = dot(jnp.where(group == c, pick4, 0.0).astype(BF), columns)
            extra = more if extra is None else extra + more
            if a == 1:
                rows = rows * scale
            rows = rows.astype(BF)
            for u in range(BATCH):
                at = pl.multiple_of(send_row(a, target(me, u, core)) + 16 * c, 16)
                big[j, pl.ds(at, 16), :] = rows[u * 16 : u * 16 + 16, :]
        if a == 1:
            extra = extra * scale4
        extra = extra.astype(BF)
        for u in range(BATCH):
            at = pl.multiple_of(send_row(a, target(me, u, core)) + 64, 16)
            big[j, pl.ds(at, 16), :] = extra[u * 16 : u * 16 + 16, :]

    def gone(j, a, core):
        def one(n, _):
            q = target(me, n, core)

            @pl.when(q != me)
            def _():
                dispatch_copy(j, a, q, me).wait_send()

            return 0

        lax.fori_loop(0, BATCH, one, 0)

    def launch(j, a, core, after=None):
        def go(n, _):
            q = target(me, n, core)
            if after is not None:
                aj, aa, ac = after
                before = target(me, n, ac)

                @pl.when(before != me)
                def _():
                    dispatch_copy(aj, aa, before, me).wait_send()

            @pl.when(q != me)
            def _():
                dispatch_copy(j, a, q, me).start()

            @pl.when(q == me)
            def _():
                own_copy(j, a).start()

            return 0

        lax.fori_loop(0, BATCH, go, 0)

    def assemble(aj, wait):
        def one(i, _):
            q = source_of(me, i)
            if wait is not None:
                wait(i, q)
            for c in range(4):
                xs[pl.ds(pl.multiple_of(q * 16, 16), 16), c * GRP : (c + 1) * GRP] = recv[
                    aj, pl.ds(pl.multiple_of(q * BLK + 16 * c, 16), 16), :
                ]
            over[pl.ds(pl.multiple_of(q * 16, 16), 16), :] = recv[
                aj, pl.ds(pl.multiple_of(q * BLK + 64, 16), 16), :
            ]
            return 0

        lax.fori_loop(0, PEERS, one, 0)
        moved = dot(perm[...], over[...]).astype(BF)
        for c in range(4):
            xs[512:640, c * GRP : (c + 1) * GRP] = moved[c * 128 : (c + 1) * 128, :]

    def arrive(j, a):
        def wait(i, q):
            @pl.when(q != me)
            def _():
                dispatch_copy(j, a, q, q).wait_recv()

            @pl.when(q == me)
            def _():
                own_copy(j, a).wait()

        assemble(2 * j + a, wait)

    def return_copy(j, q, lands):
        return pltpu.make_async_remote_copy(
            src_ref=recv.at[2 * j, block(q)],
            dst_ref=back.at[j, block(lands)],
            send_sem=r_send.at[j, q],
            recv_sem=r_recv.at[j, lands],
            device_id=(b, q),
            device_id_type=MESH,
        )

    def own_return(j):
        return pltpu.make_async_copy(recv.at[2 * j, block(me)], back.at[j, block(me)], l_sem.at[4 + j])

    def forward(j):
        arrive(j, 0)
        if j == 0:
            pl.when(core == 1)(second)

        def flip(c, _):
            at = pl.ds(pl.multiple_of(c * GRP, GRP), GRP)
            xt[at, :] = xs[:, at].T
            return 0

        lax.fori_loop(0, 4, flip, 0)
        load_in(j).wait()

        def part(n, _):
            at = pl.ds(pl.multiple_of(n * 256, 256), 256)
            g = dot(xs[...], win[:, at])
            u = dot(xs[...], win[:, pl.ds(pl.multiple_of(FF + n * 256, 256), 256)])
            gate[:, at] = g
            up[:, at] = u
            h = (g * jax.nn.sigmoid(g) * u).astype(BF)
            hid[:, at] = h
            ht[at, :] = h.T
            return 0

        lax.fori_loop(0, FF // 256, part, 0)
        if j == 0:
            load_in(1).start()
        load_out(j).wait()

        def produce(c, _):
            made = dot(hid[...], wout[:, pl.ds(pl.multiple_of(c * GRP, GRP), GRP)]).astype(BF)
            for q in range(PEERS):
                recv[2 * j, pl.ds(pl.multiple_of(q * BLK + 16 * c, 16), 16), :] = made[
                    16 * q : 16 * q + 16, :
                ]
            side[pl.ds(pl.multiple_of(c * 128, 128), 128), :] = made[512:640, :]
            return 0

        lax.fori_loop(0, 4, produce, 0)
        moved = dot(perm_t[...], side[...]).astype(BF)
        for q in range(PEERS):
            recv[2 * j, q * BLK + 64 : q * BLK + 80, :] = moved[16 * q : 16 * q + 16, :]

    def send_back(j):
        def go(i, _):
            q = source_of(me, i)

            @pl.when(q != me)
            def _():
                return_copy(j, q, me).start()

            return 0

        lax.fori_loop(0, PEERS, go, 0)
        own_return(j).start()

    def unit_rows(u, p):
        at, n = rows_of(p)
        return pl.ds(pl.multiple_of(u * UROWS + at, 128), n)

    def unit_at(j, u, p):
        at, n = rows_of(p)
        if u < 2:
            buf, row = j, u * UROWS
        elif u < 4:
            buf, row = 1 - j, (2 * AREA if j == 0 else AREA) + (u - 2) * UROWS
        else:
            buf, row = j, 2 * AREA + (u - 4) * UROWS
        return buf, pl.ds(pl.multiple_of(row + at, 128), n)

    def z_copy(j, k, p):
        return pltpu.make_async_remote_copy(
            src_ref=big.at[unit_at(j, k, p)],
            dst_ref=parts.at[j, unit_rows(k, p)],
            send_sem=z_send.at[j, k, p],
            recv_sem=z_recv.at[j, k, p],
            device_id=((right, left)[k % 2], me),
            device_id_type=MESH,
        )

    owners = ((2, 0, 1, (0, 1)), (1, 4, 2, (2,)), (3, 3, 5, (3,)), (0, 6, 7, ()))

    def put(j, p, entry, term):
        n = rows_of(p)[1]
        _, first, second, leave = entry
        for u, piece in ((first, term[0:n, :]), (second, term[n : 2 * n, :])):
            buf, at = unit_at(j, u, p)
            big[buf, at, :] = piece
        for u in leave:
            z_copy(j, u, p).start()

    def backward(j):
        arrive(j, 1)

        if j == 1:
            for a in range(2):
                gone(0, a, 1)
                gone(1, a, 0)
            each(lambda j, p: [z_copy(j, k, p).wait_send() for k in (2, 3)], 0, 0, 4)
        for entry in owners:
            o = lax.rem(b + entry[0], 4)
            put(j, 0, entry, dot(ht[...], xs[:, pl.ds(pl.multiple_of(o * GRP, GRP), GRP)]).astype(BF))
            if j == 0 and entry[0] == 2:
                pl.when(core == 0)(first_grads)

        def part(n, _):
            at = pl.ds(pl.multiple_of(n * 256, 256), 256)
            grad = dot(xs[...], wout[at, :], ((1,), (1,)))
            g = gate[:, at]
            s = jax.nn.sigmoid(g)
            gg[:, at] = (grad * up[:, at] * s * (1.0 + g * (1.0 - s))).astype(BF)
            gg[:, pl.ds(pl.multiple_of(FF + n * 256, 256), 256)] = (grad * (g * s)).astype(BF)
            return 0

        lax.fori_loop(0, FF // 256, part, 0)
        if j == 0:
            load_out(1).start()

        def unit_in(p, _):
            columns = pl.ds(pl.multiple_of((p - 1) * GRP, GRP), GRP)
            for entry in owners:
                o = lax.rem(b + entry[0], 4)
                rows = pl.ds(pl.multiple_of(o * GRP, GRP), GRP)
                put(j, p, entry, dot(xt[rows, :], gg[:, columns]).astype(BF))
            return 0

        lax.fori_loop(1, 4, unit_in, 0)

    def fetch(j, k, p, where):
        n = rows_of(p)[1]
        return pltpu.make_async_copy(
            parts.at[j, unit_rows(k, p)], stage.at[where, pl.ds(0, n)], o_sem.at[where]
        )

    def middle(j, p):
        n = rows_of(p)[1]
        for d in range(2):
            z_copy(j, d, p).wait_recv()
            fetch(j, d, p, d).start()
        for d in range(2):
            fetch(j, d, p, d).wait()
            buf, at = unit_at(j, 4 + d, p)
            both = big[buf, at, :].astype(F32) + stage[d, 0:n, :].astype(F32)
            big[buf, at, :] = both.astype(BF)
            z_copy(j, 4 + d, p).start()

    def early(j, p):
        n = rows_of(p)[1]
        for k in (3, 2):
            z_copy(j, k, p).wait_recv()
            fetch(j, k, p, k).start()
        for h in range(2):
            fetch(j, 3 - h, p, 3 - h).wait()
            buf, at = unit_at(j, 6 + h, p)
            both = big[buf, at, :].astype(F32) + stage[3 - h, 0:n, :].astype(F32)
            big[buf, at, :] = both.astype(BF)

    def result_copy(j, h, p):
        if isinstance(p, int):
            to = gout.at[j, pl.ds(384 * h, 384)]
        else:
            to = gin.at[j, pl.ds(256 * h, 256), pl.ds(pl.multiple_of((p - 1) * GRP, GRP), GRP)]
        return pltpu.make_async_copy(big.at[unit_at(j, 6 + h, p)], to, g_sem.at[j, h, p])

    def finish(j, p):
        n = rows_of(p)[1]
        for h in range(2):
            z_copy(j, 4 + h, p).wait_recv()
            fetch(j, 4 + h, p, h).start()
        for h in range(2):
            fetch(j, 4 + h, p, h).wait()
            buf, at = unit_at(j, 6 + h, p)
            whole = big[buf, at, :].astype(F32) + stage[h, 0:n, :].astype(F32)
            big[buf, at, :] = whole.astype(BF)
            result_copy(j, h, p).start()

    def each(fn, j, lo, hi):
        if lo == 0:
            fn(j, 0)

        def one(p, _):
            fn(j, p)
            return 0

        lax.fori_loop(max(lo, 1), hi, one, 0)

    def combine(j):
        def take(q):
            return pltpu.make_async_copy(
                back.at[j, block(q)], recv.at[2 * j + 1, block(q)], b_sem.at[q]
            )

        own_return(j).wait()
        take(me).start()

        def arrived(i, _):
            q = peer(me, i)
            return_copy(j, q, q).wait_recv()
            take(q).start()
            return 0

        lax.fori_loop(1, PEERS, arrived, 0)
        assemble(2 * j + 1, lambda i, q: take(q).wait())
        mine = slot[j * PEERS : (j + 1) * PEERS, :]
        heavy = wgt[j * PEERS : (j + 1) * PEERS, :]
        for s in range(4):
            slot4[pl.ds(s, PEERS, stride=4), :] = mine
            wgt4[pl.ds(s, PEERS, stride=4), :] = heavy
        sub = iota((PEERS, MAIN, TOK), 1).astype(F32)
        hot = jnp.where(jnp.broadcast_to(mine[:, None, :], (PEERS, MAIN, TOK)) == sub, 1.0, 0.0)
        hot_w = (hot * heavy[:, None, :]).reshape(512, TOK)
        hot = hot.reshape(512, TOK)
        tail = (16 + lax.rem(iota((128, TOK), 0), 4)).astype(F32)
        hot4 = jnp.where(slot4[...] == tail, 1.0, 0.0)
        hot4_w = hot4 * wgt4[...]
        dots = dot(xs[...], cot[...], ((1,), (1,)))
        near = jnp.sum((dots[0:512, :] * hot).reshape(PEERS, MAIN, TOK), axis=1)
        slot4[...] = dots[512:640, :] * hot4
        for s in range(4):
            near = near + slot4[pl.ds(s, PEERS, stride=4), :]
        aff[j * PEERS : (j + 1) * PEERS, :] = near
        mix_t = jnp.concatenate([hot_w.T, hot4_w.T], axis=1).astype(BF)
        for c in range(4):
            at = slice(c * GRP, (c + 1) * GRP)
            made = dot(mix_t, xs[:, at])
            if j == 0:
                macc[:, at] = made
            else:
                mixed[:, at] = (macc[:, at] + made).astype(BF)

    core = lax.rem(me, 2)

    def first():
        launch(0, 0, 1, (0, 1, 0))

    def first_grads():
        launch(0, 1, 1)

    def second():
        for target_core in range(2):
            for a in range(2):
                launch(1, a, target_core)

    make(0, 0, 0)
    pl.semaphore_wait(barrier, PEERS + 1)
    launch(0, 0, 0)
    make(0, 1, 0)

    r0, r1 = iota((GRP, GRP), 0), iota((GRP, GRP), 1)

    def place(m):
        r = lax.rem(m, 128)
        return 16 * lax.div(r, 4) + 4 * lax.div(m, 128) + lax.rem(r, 4)

    perm[...] = jnp.where(r1 == place(r0), 1.0, 0.0).astype(BF)
    perm_t[...] = jnp.where(r0 == place(r1), 1.0, 0.0).astype(BF)

    for a in range(2):
        make(0, a, 1)
    for target_core in range(2):
        for a in range(2):
            make(1, a, target_core)
    launch(0, 1, 0, (0, 0, 0))
    pl.when(core == 1)(first)
    pl.when(core == 1)(first_grads)
    forward(0)
    pl.when(core == 0)(first)
    backward(0)
    pl.when(core == 0)(second)
    each(middle, 0, 0, 4)
    forward(1)
    backward(1)
    send_back(0)
    send_back(1)

    def between(j, p):
        middle(1, p)
        early(0, p)
        finish(0, p)

    each(between, 0, 0, 4)
    each(early, 1, 0, 4)
    combine(0)
    each(finish, 1, 0, 2)
    combine(1)
    found = []
    for k in range(8):
        found.append(
            jnp.sum(jnp.where(ids[k : k + 1, :] == expert, aff[...], 0.0), axis=0, keepdims=True)
        )
    affinity = jnp.concatenate(found, axis=0)
    score[...] = (affinity - jnp.sum(weights * affinity, axis=0, keepdims=True)) / total

    each(finish, 1, 2, 4)
    for a in range(2):
        gone(1, a, 1)

    def returned(i, _):
        q = peer(me, i)
        for j in range(2):
            return_copy(j, q, q).wait_send()
        return 0

    lax.fori_loop(1, PEERS, returned, 0)

    def last(j, p):
        for k in range(6):
            if j == 1 or k not in (2, 3):
                z_copy(j, k, p).wait_send()
        for h in range(2):
            result_copy(j, h, p).wait()

    each(last, 0, 0, 4)
    each(last, 1, 0, 4)


def shards(tokens, expert_ids, gate_scores, w_in, w_out, cotangent):
    vm = pl.BlockSpec(memory_space=pltpu.VMEM)
    anywhere = pl.BlockSpec(memory_space=pl.ANY)
    mixed, score_t, grad_in, grad_out, _, _ = pl.pallas_call(
        kernel,
        out_shape=[
            jax.ShapeDtypeStruct((TOK, D), BF),
            jax.ShapeDtypeStruct((8, TOK), F32),
            jax.ShapeDtypeStruct((2, 512, 2 * FF), BF),
            jax.ShapeDtypeStruct((2, FF, 512), BF),
            jax.ShapeDtypeStruct((2, AREA, GRP), BF),
            jax.ShapeDtypeStruct((2, 6 * UROWS, GRP), BF),
        ],
        in_specs=[vm, vm, vm, vm, anywhere, anywhere],
        out_specs=[vm, vm, anywhere, anywhere, anywhere, anywhere],
        scratch_shapes=[
            pltpu.VMEM((2, 2 * AREA + 4 * UROWS, GRP), BF),
            pltpu.VMEM((4, AREA, GRP), BF),
            pltpu.VMEM((D, 2 * FF), BF),
            pltpu.VMEM((FF, D), BF),
            pltpu.VMEM((ROWS, D), BF),
            pltpu.VMEM((D, ROWS), BF),
            pltpu.VMEM((FF, ROWS), BF),
            pltpu.VMEM((ROWS, FF), BF),
            pltpu.VMEM((ROWS, FF), F32),
            pltpu.VMEM((ROWS, FF), F32),
            pltpu.VMEM((ROWS, 2 * FF), BF),
            pltpu.VMEM((4, 384, GRP), BF),
            pltpu.VMEM((64, TOK), F32),
            pltpu.VMEM((64, TOK), F32),
            pltpu.VMEM((8, TOK), F32),
            pltpu.VMEM((GRP, GRP), BF),
            pltpu.VMEM((GRP, GRP), BF),
            pltpu.VMEM((GRP, GRP), BF),
            pltpu.VMEM((GRP, GRP), BF),
            pltpu.VMEM((128, TOK), F32),
            pltpu.VMEM((128, TOK), F32),
            pltpu.VMEM((64, TOK), F32),
            pltpu.VMEM((TOK, D), F32),
            pltpu.SemaphoreType.DMA((4, PEERS)),
            pltpu.SemaphoreType.DMA((4, PEERS)),
            pltpu.SemaphoreType.DMA((2, PEERS)),
            pltpu.SemaphoreType.DMA((2, PEERS)),
            pltpu.SemaphoreType.DMA((2, 6, 4)),
            pltpu.SemaphoreType.DMA((2, 6, 4)),
            pltpu.SemaphoreType.DMA((7,)),
            pltpu.SemaphoreType.DMA((2,)),
            pltpu.SemaphoreType.DMA((4,)),
            pltpu.SemaphoreType.DMA((2, 2, 4)),
            pltpu.SemaphoreType.DMA((PEERS,)),
        ],
        compiler_params=pltpu.CompilerParams(
            collective_id=0, has_side_effects=True, vmem_limit_bytes=63 * 2**20
        ),
        cost_estimate=pl.CostEstimate(
            flops=28_000_000_000, bytes_accessed=60_000_000, transcendentals=2_000_000
        ),
    )(tokens, cotangent, expert_ids.T, gate_scores.T, w_in, w_out)
    return (mixed, score_t.T, grad_in, grad_out)


def solution(mesh):
    in_specs = (
        P(("dp", "expert"), None),
        P(("dp", "expert"), None),
        P(("dp", "expert"), None),
        P("expert", None, None),
        P("expert", None, None),
        P(("dp", "expert"), None),
    )
    out_specs = (
        P(("dp", "expert"), None),
        P(("dp", "expert"), None),
        P("expert", "dp", None),
        P("expert", None, "dp"),
    )
    return jax.shard_map(shards, mesh=mesh, in_specs=in_specs, out_specs=out_specs, check_vma=False)
```

```python
import functools

import jax
import jax.numpy as jnp
from jax import lax
from jax.experimental import pallas as pl
from jax.experimental.pallas import tpu as pltpu
from jax.sharding import PartitionSpec as P

MESH = pl.DeviceIdType.MESH
BF = jnp.bfloat16
F32 = jnp.float32

TOK = 128
D = 2048
FF = 768
PEERS = 32
MAIN = 16
GRP = 512
BLK = 80
ROWS = PEERS * 20
AREA = PEERS * BLK
UROWS = 384 + 3 * 256
BATCH = 16


def dot(a, b, dims=((1,), (0,))):
    return lax.dot_general(a, b, (dims, ((), ())), preferred_element_type=F32)


def peer(me, i):
    c = lax.rem(me, 2)
    x = lax.rem(lax.div(me, 2), 4)
    y = lax.div(me, 8)
    dc = lax.rem(i, 2)
    dx = lax.rem(lax.div(i, 2), 4)
    dy = lax.div(i, 8)
    return lax.rem(y + dy, 4) * 8 + lax.rem(x + dx, 4) * 2 + lax.rem(c + dc, 2)


def chip(me, n, sign):
    k = lax.rem(n * 7, BATCH)
    x = lax.rem(lax.div(me, 2), 4) + 4 + sign * lax.rem(k, 4)
    y = lax.div(me, 8) + 4 + sign * lax.div(k, 4)
    return lax.rem(y, 4) * 4 + lax.rem(x, 4)


def target(me, n, core):
    return 2 * chip(me, n, 1) + core


def source_of(me, i):
    return 2 * chip(me, lax.div(i, 2), -1) + lax.rem(i, 2)


def iota(shape, dim):
    return lax.broadcasted_iota(jnp.int32, shape, dim)


def rows_of(p):
    if isinstance(p, int):
        return (0, 384) if p == 0 else (384 + 256 * (p - 1), 256)
    return (pl.multiple_of(384 + 256 * (p - 1), 128), 256)


def kernel(
    tok, cot, ids, scores, win_hbm, wout_hbm,
    mixed, score, gin, gout, back, parts,
    big, recv, win, wout, xs, xt, ht, hid, gate, up, gg, stage, slot, wgt, cut, perm, perm_t,
    over, side, slot4, wgt4, aff, macc,
    d_send, d_recv, r_send, r_recv, z_send, z_recv, l_sem, w_sem, o_sem, g_sem, b_sem,
):
    b = lax.axis_index("dp")
    me = lax.axis_index("expert")
    right = lax.rem(b + 1, 4)
    left = lax.rem(b + 3, 4)

    def load_in(j):
        return pltpu.make_async_copy(win_hbm.at[j], win, w_sem.at[0])

    def load_out(j):
        return pltpu.make_async_copy(wout_hbm.at[j], wout, w_sem.at[1])

    load_in(0).start()
    load_out(0).start()

    barrier = pltpu.get_barrier_semaphore()

    def greet(i, _):
        pl.semaphore_signal(barrier, inc=1, device_id=(b, peer(me, i)), device_id_type=MESH)
        return 0

    lax.fori_loop(1, PEERS, greet, 0)
    pl.semaphore_signal(barrier, inc=1, device_id=(right, me), device_id_type=MESH)
    pl.semaphore_signal(barrier, inc=1, device_id=(left, me), device_id_type=MESH)

    names = ids[...]
    total = jnp.sum(scores[...], axis=0, keepdims=True)
    weights = scores[...] / total
    row = iota((64, TOK), 0)
    expert = 2 * lax.rem(row, PEERS) + lax.div(row, PEERS)
    member = jnp.zeros((64, TOK), F32)
    weight = jnp.zeros((64, TOK), F32)
    for k in range(8):
        hit = names[k : k + 1, :] == expert
        member = member + jnp.where(hit, 1.0, 0.0)
        weight = weight + jnp.where(hit, weights[k : k + 1, :], 0.0)
    earlier = jnp.where(iota((TOK, TOK), 0) < iota((TOK, TOK), 1), 1.0, 0.0).astype(BF)
    slot[...] = jnp.where(member > 0.0, dot(member.astype(BF), earlier), -1.0)
    wgt[...] = weight

    r0, r1 = iota((GRP, GRP), 0), iota((GRP, GRP), 1)

    def place(m):
        r = lax.rem(m, 128)
        return 16 * lax.div(r, 4) + 4 * lax.div(m, 128) + lax.rem(r, 4)

    perm[...] = jnp.where(r1 == place(r0), 1.0, 0.0).astype(BF)
    perm_t[...] = jnp.where(r0 == place(r1), 1.0, 0.0).astype(BF)

    main_slot = iota((MAIN, TOK), 0).astype(F32)
    over_row = iota((MAIN, TOK), 0)
    over_slot = (16 + lax.rem(over_row, 4)).astype(F32)
    group = lax.rem(lax.div(iota((BATCH * MAIN, TOK), 0), 4), 4)

    def block(q):
        return pl.ds(pl.multiple_of(q * BLK, 16), BLK)

    def send_row(a, q):
        return lax.rem(q, 2) * AREA + a * (AREA // 2) + lax.div(q, 2) * BLK

    def send_block(j, a, q):
        return big.at[j, pl.ds(pl.multiple_of(send_row(a, q), 16), BLK)]

    def dispatch_copy(j, a, q, lands):
        return pltpu.make_async_remote_copy(
            src_ref=send_block(j, a, q),
            dst_ref=recv.at[2 * j + a, block(lands)],
            send_sem=d_send.at[2 * j + a, q],
            recv_sem=d_recv.at[2 * j + a, lands],
            device_id=(b, q),
            device_id_type=MESH,
        )

    def own_copy(j, a):
        return pltpu.make_async_copy(
            send_block(j, a, me), recv.at[2 * j + a, block(me)], l_sem.at[2 * j + a]
        )

    def make(j, a, core):
        source = (tok, cot)[a]
        hots, overs, w_main, w_over = [], [], [], []
        for u in range(BATCH):
            q = target(me, u, core)
            mine = slot[pl.ds(j * PEERS + q, 1), :]
            hot = jnp.where(main_slot == mine, 1.0, 0.0)
            hot4 = jnp.where(over_slot == mine, 1.0, 0.0)
            hots.append(hot)
            overs.append(hot4)
            if a == 1:
                heavy = wgt[pl.ds(j * PEERS + q, 1), :]
                w_main.append(jnp.sum(hot * heavy, axis=1, keepdims=True))
                w_over.append(jnp.sum(hot4 * heavy, axis=1, keepdims=True))
        pick = jnp.concatenate(hots, axis=0).astype(BF)
        pick4 = jnp.concatenate(overs, axis=0)
        scale = jnp.concatenate(w_main, axis=0) if a == 1 else None
        scale4 = jnp.concatenate(w_over, axis=0) if a == 1 else None
        extra = None
        for c in range(4):
            columns = source[:, c * GRP : (c + 1) * GRP]
            rows = dot(pick, columns)
            more = dot(jnp.where(group == c, pick4, 0.0).astype(BF), columns)
            extra = more if extra is None else extra + more
            if a == 1:
                rows = rows * scale
            rows = rows.astype(BF)
            for u in range(BATCH):
                at = pl.multiple_of(send_row(a, target(me, u, core)) + 16 * c, 16)
                big[j, pl.ds(at, 16), :] = rows[u * 16 : u * 16 + 16, :]
        if a == 1:
            extra = extra * scale4
        extra = extra.astype(BF)
        for u in range(BATCH):
            at = pl.multiple_of(send_row(a, target(me, u, core)) + 64, 16)
            big[j, pl.ds(at, 16), :] = extra[u * 16 : u * 16 + 16, :]

    def gone(j, a, core):
        def one(n, _):
            q = target(me, n, core)

            @pl.when(q != me)
            def _():
                dispatch_copy(j, a, q, me).wait_send()

            return 0

        lax.fori_loop(0, BATCH, one, 0)

    def launch(j, a, core, after=None):
        def go(n, _):
            q = target(me, n, core)
            if after is not None:
                aj, aa, ac = after
                before = target(me, n, ac)

                @pl.when(before != me)
                def _():
                    dispatch_copy(aj, aa, before, me).wait_send()

            @pl.when(q != me)
            def _():
                dispatch_copy(j, a, q, me).start()

            @pl.when(q == me)
            def _():
                own_copy(j, a).start()

            return 0

        lax.fori_loop(0, BATCH, go, 0)

    def assemble(aj, wait):
        def one(i, _):
            q = source_of(me, i)
            if wait is not None:
                wait(i, q)
            for c in range(4):
                xs[pl.ds(pl.multiple_of(q * 16, 16), 16), c * GRP : (c + 1) * GRP] = recv[
                    aj, pl.ds(pl.multiple_of(q * BLK + 16 * c, 16), 16), :
                ]
            over[pl.ds(pl.multiple_of(q * 16, 16), 16), :] = recv[
                aj, pl.ds(pl.multiple_of(q * BLK + 64, 16), 16), :
            ]
            return 0

        lax.fori_loop(0, PEERS, one, 0)
        moved = dot(perm[...], over[...]).astype(BF)
        for c in range(4):
            xs[512:640, c * GRP : (c + 1) * GRP] = moved[c * 128 : (c + 1) * 128, :]

    def arrive(j, a):
        def wait(i, q):
            @pl.when(q != me)
            def _():
                dispatch_copy(j, a, q, q).wait_recv()

            @pl.when(q == me)
            def _():
                own_copy(j, a).wait()

        assemble(2 * j + a, wait)

    def return_copy(j, q, lands):
        return pltpu.make_async_remote_copy(
            src_ref=recv.at[2 * j, block(q)],
            dst_ref=back.at[j, block(lands)],
            send_sem=r_send.at[j, q],
            recv_sem=r_recv.at[j, lands],
            device_id=(b, q),
            device_id_type=MESH,
        )

    def own_return(j):
        return pltpu.make_async_copy(recv.at[2 * j, block(me)], back.at[j, block(me)], l_sem.at[4 + j])

    def forward(j):
        arrive(j, 0)
        if j == 0:
            pl.when(core == 1)(second)

        def flip(c, _):
            at = pl.ds(pl.multiple_of(c * GRP, GRP), GRP)
            xt[at, :] = xs[:, at].T
            return 0

        lax.fori_loop(0, 4, flip, 0)
        load_in(j).wait()

        def part(n, _):
            at = pl.ds(pl.multiple_of(n * 256, 256), 256)
            g = dot(xs[...], win[:, at])
            u = dot(xs[...], win[:, pl.ds(pl.multiple_of(FF + n * 256, 256), 256)])
            gate[:, at] = g
            up[:, at] = u
            h = (g * jax.nn.sigmoid(g) * u).astype(BF)
            hid[:, at] = h
            ht[at, :] = h.T
            return 0

        lax.fori_loop(0, FF // 256, part, 0)
        if j == 0:
            load_in(1).start()
        load_out(j).wait()

        def produce(c, _):
            made = dot(hid[...], wout[:, pl.ds(pl.multiple_of(c * GRP, GRP), GRP)]).astype(BF)
            for q in range(PEERS):
                recv[2 * j, pl.ds(pl.multiple_of(q * BLK + 16 * c, 16), 16), :] = made[
                    16 * q : 16 * q + 16, :
                ]
            side[pl.ds(pl.multiple_of(c * 128, 128), 128), :] = made[512:640, :]
            return 0

        lax.fori_loop(0, 4, produce, 0)
        moved = dot(perm_t[...], side[...]).astype(BF)
        for q in range(PEERS):
            recv[2 * j, q * BLK + 64 : q * BLK + 80, :] = moved[16 * q : 16 * q + 16, :]

    def send_back(j):
        def go(i, _):
            q = source_of(me, i)

            @pl.when(q != me)
            def _():
                return_copy(j, q, me).start()

            return 0

        lax.fori_loop(0, PEERS, go, 0)
        own_return(j).start()

    def unit_rows(u, p):
        at, n = rows_of(p)
        return pl.ds(pl.multiple_of(u * UROWS + at, 128), n)

    def unit_at(j, u, p):
        at, n = rows_of(p)
        if u < 2:
            buf, row = j, u * UROWS
        elif u < 4:
            buf, row = 1 - j, (2 * AREA if j == 0 else AREA) + (u - 2) * UROWS
        else:
            buf, row = j, 2 * AREA + (u - 4) * UROWS
        return buf, pl.ds(pl.multiple_of(row + at, 128), n)

    def z_copy(j, k, p):
        return pltpu.make_async_remote_copy(
            src_ref=big.at[unit_at(j, k, p)],
            dst_ref=parts.at[j, unit_rows(k, p)],
            send_sem=z_send.at[j, k, p],
            recv_sem=z_recv.at[j, k, p],
            device_id=((right, left)[k % 2], me),
            device_id_type=MESH,
        )

    owners = ((2, 0, 1, (0, 1)), (1, 4, 2, (2,)), (3, 3, 5, (3,)), (0, 6, 7, ()))

    def put(j, p, entry, term):
        n = rows_of(p)[1]
        _, first, second, leave = entry
        for u, piece in ((first, term[0:n, :]), (second, term[n : 2 * n, :])):
            buf, at = unit_at(j, u, p)
            big[buf, at, :] = piece
        for u in leave:
            z_copy(j, u, p).start()

    def backward(j):
        arrive(j, 1)

        if j == 1:
            for a in range(2):
                gone(0, a, 1)
                gone(1, a, 0)
            each(lambda j, p: [z_copy(j, k, p).wait_send() for k in (2, 3)], 0, 0, 4)
        for entry in owners:
            o = lax.rem(b + entry[0], 4)
            put(j, 0, entry, dot(ht[...], xs[:, pl.ds(pl.multiple_of(o * GRP, GRP), GRP)]).astype(BF))

        def part(n, _):
            at = pl.ds(pl.multiple_of(n * 256, 256), 256)
            grad = dot(xs[...], wout[at, :], ((1,), (1,)))
            g = gate[:, at]
            s = jax.nn.sigmoid(g)
            gg[:, at] = (grad * up[:, at] * s * (1.0 + g * (1.0 - s))).astype(BF)
            gg[:, pl.ds(pl.multiple_of(FF + n * 256, 256), 256)] = (grad * (g * s)).astype(BF)
            return 0

        lax.fori_loop(0, FF // 256, part, 0)
        if j == 0:
            load_out(1).start()

        def unit_in(p, _):
            columns = pl.ds(pl.multiple_of((p - 1) * GRP, GRP), GRP)
            for entry in owners:
                o = lax.rem(b + entry[0], 4)
                rows = pl.ds(pl.multiple_of(o * GRP, GRP), GRP)
                put(j, p, entry, dot(xt[rows, :], gg[:, columns]).astype(BF))
            return 0

        lax.fori_loop(1, 4, unit_in, 0)

    def fetch(j, k, p, where):
        n = rows_of(p)[1]
        return pltpu.make_async_copy(
            parts.at[j, unit_rows(k, p)], stage.at[where, pl.ds(0, n)], o_sem.at[where]
        )

    def middle(j, p):
        n = rows_of(p)[1]
        for d in range(2):
            z_copy(j, d, p).wait_recv()
            fetch(j, d, p, d).start()
        for d in range(2):
            fetch(j, d, p, d).wait()
            buf, at = unit_at(j, 4 + d, p)
            both = big[buf, at, :].astype(F32) + stage[d, 0:n, :].astype(F32)
            big[buf, at, :] = both.astype(BF)
            z_copy(j, 4 + d, p).start()

    def early(j, p):
        n = rows_of(p)[1]
        for k in (3, 2):
            z_copy(j, k, p).wait_recv()
            fetch(j, k, p, k).start()
        for h in range(2):
            fetch(j, 3 - h, p, 3 - h).wait()
            buf, at = unit_at(j, 6 + h, p)
            both = big[buf, at, :].astype(F32) + stage[3 - h, 0:n, :].astype(F32)
            big[buf, at, :] = both.astype(BF)

    def result_copy(j, h, p):
        if isinstance(p, int):
            to = gout.at[j, pl.ds(384 * h, 384)]
        else:
            to = gin.at[j, pl.ds(256 * h, 256), pl.ds(pl.multiple_of((p - 1) * GRP, GRP), GRP)]
        return pltpu.make_async_copy(big.at[unit_at(j, 6 + h, p)], to, g_sem.at[j, h, p])

    def finish(j, p):
        n = rows_of(p)[1]
        for h in range(2):
            z_copy(j, 4 + h, p).wait_recv()
            fetch(j, 4 + h, p, h).start()
        for h in range(2):
            fetch(j, 4 + h, p, h).wait()
            buf, at = unit_at(j, 6 + h, p)
            whole = big[buf, at, :].astype(F32) + stage[h, 0:n, :].astype(F32)
            big[buf, at, :] = whole.astype(BF)
            result_copy(j, h, p).start()

    def each(fn, j, lo, hi):
        if lo == 0:
            fn(j, 0)

        def one(p, _):
            fn(j, p)
            return 0

        lax.fori_loop(max(lo, 1), hi, one, 0)

    def combine(j):
        def take(q):
            return pltpu.make_async_copy(
                back.at[j, block(q)], recv.at[2 * j + 1, block(q)], b_sem.at[q]
            )

        own_return(j).wait()
        take(me).start()

        def arrived(i, _):
            q = peer(me, i)
            return_copy(j, q, q).wait_recv()
            take(q).start()
            return 0

        lax.fori_loop(1, PEERS, arrived, 0)
        assemble(2 * j + 1, lambda i, q: take(q).wait())
        mine = slot[j * PEERS : (j + 1) * PEERS, :]
        heavy = wgt[j * PEERS : (j + 1) * PEERS, :]
        for s in range(4):
            slot4[pl.ds(s, PEERS, stride=4), :] = mine
            wgt4[pl.ds(s, PEERS, stride=4), :] = heavy
        sub = iota((PEERS, MAIN, TOK), 1).astype(F32)
        hot = jnp.where(jnp.broadcast_to(mine[:, None, :], (PEERS, MAIN, TOK)) == sub, 1.0, 0.0)
        hot_w = (hot * heavy[:, None, :]).reshape(512, TOK)
        hot = hot.reshape(512, TOK)
        tail = (16 + lax.rem(iota((128, TOK), 0), 4)).astype(F32)
        hot4 = jnp.where(slot4[...] == tail, 1.0, 0.0)
        hot4_w = hot4 * wgt4[...]
        dots = dot(xs[...], cot[...], ((1,), (1,)))
        near = jnp.sum((dots[0:512, :] * hot).reshape(PEERS, MAIN, TOK), axis=1)
        slot4[...] = dots[512:640, :] * hot4
        for s in range(4):
            near = near + slot4[pl.ds(s, PEERS, stride=4), :]
        aff[j * PEERS : (j + 1) * PEERS, :] = near
        mix_t = jnp.concatenate([hot_w.T, hot4_w.T], axis=1).astype(BF)
        for c in range(4):
            at = slice(c * GRP, (c + 1) * GRP)
            made = dot(mix_t, xs[:, at])
            if j == 0:
                macc[:, at] = made
            else:
                mixed[:, at] = (macc[:, at] + made).astype(BF)

    core = lax.rem(me, 2)

    def first():
        launch(0, 0, 1, (0, 1, 0))
        launch(0, 1, 1)

    def second():
        for target_core in range(2):
            for a in range(2):
                launch(1, a, target_core)

    make(0, 0, 0)
    pl.semaphore_wait(barrier, PEERS + 1)
    launch(0, 0, 0)
    for a, target_core in ((1, 0), (0, 1), (1, 1)):
        make(0, a, target_core)
    launch(0, 1, 0, (0, 0, 0))

    def second_blocks():
        for target_core in range(2):
            for a in range(2):
                make(1, a, target_core)

    pl.when(core == 1)(first)
    pl.when(core == 1)(second_blocks)
    forward(0)
    pl.when(core == 0)(first)
    backward(0)
    pl.when(core == 0)(second_blocks)
    pl.when(core == 0)(second)
    each(middle, 0, 0, 4)
    forward(1)
    backward(1)
    send_back(0)
    send_back(1)

    def between(j, p):
        middle(1, p)
        early(0, p)
        finish(0, p)

    each(between, 0, 0, 4)
    each(early, 1, 0, 4)
    combine(0)
    each(finish, 1, 0, 2)
    combine(1)
    found = []
    for k in range(8):
        found.append(
            jnp.sum(jnp.where(ids[k : k + 1, :] == expert, aff[...], 0.0), axis=0, keepdims=True)
        )
    affinity = jnp.concatenate(found, axis=0)
    score[...] = (affinity - jnp.sum(weights * affinity, axis=0, keepdims=True)) / total

    each(finish, 1, 2, 4)
    for a in range(2):
        gone(1, a, 1)

    def returned(i, _):
        q = peer(me, i)
        for j in range(2):
            return_copy(j, q, q).wait_send()
        return 0

    lax.fori_loop(1, PEERS, returned, 0)

    def last(j, p):
        for k in range(6):
            if j == 1 or k not in (2, 3):
                z_copy(j, k, p).wait_send()
        for h in range(2):
            result_copy(j, h, p).wait()

    each(last, 0, 0, 4)
    each(last, 1, 0, 4)


def shards(tokens, expert_ids, gate_scores, w_in, w_out, cotangent):
    vm = pl.BlockSpec(memory_space=pltpu.VMEM)
    anywhere = pl.BlockSpec(memory_space=pl.ANY)
    mixed, score_t, grad_in, grad_out, _, _ = pl.pallas_call(
        kernel,
        out_shape=[
            jax.ShapeDtypeStruct((TOK, D), BF),
            jax.ShapeDtypeStruct((8, TOK), F32),
            jax.ShapeDtypeStruct((2, 512, 2 * FF), BF),
            jax.ShapeDtypeStruct((2, FF, 512), BF),
            jax.ShapeDtypeStruct((2, AREA, GRP), BF),
            jax.ShapeDtypeStruct((2, 6 * UROWS, GRP), BF),
        ],
        in_specs=[vm, vm, vm, vm, anywhere, anywhere],
        out_specs=[vm, vm, anywhere, anywhere, anywhere, anywhere],
        scratch_shapes=[
            pltpu.VMEM((2, 2 * AREA + 4 * UROWS, GRP), BF),
            pltpu.VMEM((4, AREA, GRP), BF),
            pltpu.VMEM((D, 2 * FF), BF),
            pltpu.VMEM((FF, D), BF),
            pltpu.VMEM((ROWS, D), BF),
            pltpu.VMEM((D, ROWS), BF),
            pltpu.VMEM((FF, ROWS), BF),
            pltpu.VMEM((ROWS, FF), BF),
            pltpu.VMEM((ROWS, FF), F32),
            pltpu.VMEM((ROWS, FF), F32),
            pltpu.VMEM((ROWS, 2 * FF), BF),
            pltpu.VMEM((4, 384, GRP), BF),
            pltpu.VMEM((64, TOK), F32),
            pltpu.VMEM((64, TOK), F32),
            pltpu.VMEM((8, TOK), F32),
            pltpu.VMEM((GRP, GRP), BF),
            pltpu.VMEM((GRP, GRP), BF),
            pltpu.VMEM((GRP, GRP), BF),
            pltpu.VMEM((GRP, GRP), BF),
            pltpu.VMEM((128, TOK), F32),
            pltpu.VMEM((128, TOK), F32),
            pltpu.VMEM((64, TOK), F32),
            pltpu.VMEM((TOK, D), F32),
            pltpu.SemaphoreType.DMA((4, PEERS)),
            pltpu.SemaphoreType.DMA((4, PEERS)),
            pltpu.SemaphoreType.DMA((2, PEERS)),
            pltpu.SemaphoreType.DMA((2, PEERS)),
            pltpu.SemaphoreType.DMA((2, 6, 4)),
            pltpu.SemaphoreType.DMA((2, 6, 4)),
            pltpu.SemaphoreType.DMA((7,)),
            pltpu.SemaphoreType.DMA((2,)),
            pltpu.SemaphoreType.DMA((4,)),
            pltpu.SemaphoreType.DMA((2, 2, 4)),
            pltpu.SemaphoreType.DMA((PEERS,)),
        ],
        compiler_params=pltpu.CompilerParams(
            collective_id=0, has_side_effects=True, vmem_limit_bytes=63 * 2**20
        ),
        cost_estimate=pl.CostEstimate(
            flops=28_000_000_000, bytes_accessed=60_000_000, transcendentals=2_000_000
        ),
    )(tokens, cotangent, expert_ids.T, gate_scores.T, w_in, w_out)
    return (mixed, score_t.T, grad_in, grad_out)


def solution(mesh):
    in_specs = (
        P(("dp", "expert"), None),
        P(("dp", "expert"), None),
        P(("dp", "expert"), None),
        P("expert", None, None),
        P("expert", None, None),
        P(("dp", "expert"), None),
    )
    out_specs = (
        P(("dp", "expert"), None),
        P(("dp", "expert"), None),
        P("expert", "dp", None),
        P("expert", None, "dp"),
    )
    return jax.shard_map(shards, mesh=mesh, in_specs=in_specs, out_specs=out_specs, check_vma=False)
```
